32 devices in a mesh: groups: 2 (over y), row: 4 (over x, core), col: 4 (over z).
Axes of the slice: x: 2, y: 2, z: 4, core: 2. Of those that a mesh axis runs over, the one named last changes fastest.
Arguments:
- a_blocks: float32 [8, 4, 2, 384, 384], P(('groups', 'col'), 'row'), parts along dimension 0, may hold values from -0.3125 to 0.3125
- first_factor_cell_index: int32 [8, 4, 2], P(('groups', 'col'), 'row'), parts along dimension 0, may hold values from 0 to 48, as said below
- b_blocks: float32 [8, 4, 2, 384, 384], P(('groups', 'col'), 'row'), parts along dimension 0, may hold values from -6 to 6
- second_factor_cell_index: int32 [8, 4, 2], P(('groups', 'col'), 'row'), parts along dimension 0, may hold values from 0 to 48, as said below
- c_where: int32 [8, 4, 2], P(('groups', 'col'), 'row'), parts along dimension 0, may hold values from 0 to 48, as said below
Outputs:
- c_blocks: float32 [8, 4, 2, 384, 384], P(('groups', 'col'), 'row'), parts along dimension 0
The draws below stay inside these ranges and needn't reach their ends.
There are 2 independent parts, one for each index of `groups`. The reference program is written for one: setup_inputs(seed, part) draws one part's arguments, and reference() takes and returns one part's arrays. A program takes and returns all parts, laid end to end along the dimension named above; each array names one. Nothing has to cross between parts.
Inputs may be any that keep to these rules, and one draw needn't show every extreme that they name: `first_factor_cell_index`: each value is a cell r * 7 + c of a 7 x 7 tile; the 2 cells of one tile are distinct. `second_factor_cell_index`: each value is a cell r * 7 + c of a 7 x 7 tile; the 2 cells of one tile are distinct. `c_where`: each value is a cell r * 7 + c of a 7 x 7 tile; the 2 cells of one tile are distinct.
All inputs are finite; a program needn't handle non-finite values.
Results may differ from the reference program's by a relative error of at most 0.0003.
Values sent between devices are 32-bit elements; how exact they have to be, the bound alone decides.
No kernel may reach another device: no remote copies, remote signals or barrier semaphores. Data moves between devices by JAX's collectives and lax.ppermute only.
A program may use at most 64 MiB of HBM per device.

```python
import jax
import jax.numpy as jnp
from jax import lax

BLOCK = 384
TILE = 7
SLOTS = 2
STEPS = 3
N_ROW = 4
N_COL = 4


def select_cell_positions(random_split_key, extra_cell_picks):
    cell_positions = TILE * TILE
    scores = jax.random.randint(random_split_key, (N_ROW, N_ROW, cell_positions), 0, 1 << 20)
    sorted_scores = scores * cell_positions + jnp.arange(cell_positions, dtype=jnp.int32)[None, None, :]
    sorted_scores = sorted_scores + extra_cell_picks
    return lax.top_k(sorted_scores, SLOTS)[1].astype(jnp.int32)


def pattern_tables(key):
    cell_positions = TILE * TILE
    extra_cell_picks = jnp.zeros((N_ROW, N_ROW, cell_positions), jnp.int32)
    extra_cell_picks = extra_cell_picks.at[0, 0, 0].set(1 << 27).at[0, 0, cell_positions - 1].set(1 << 27)
    first_factor_cell_index = select_cell_positions(jax.random.fold_in(key, 101), extra_cell_picks)
    second_factor_cell_index = select_cell_positions(jax.random.fold_in(key, 202), extra_cell_picks)
    tile_rows = jnp.arange(N_ROW, dtype=jnp.int32)[:, None]
    tile_cols = jnp.arange(N_ROW, dtype=jnp.int32)[None, :]
    every_cell = jnp.arange(cell_positions, dtype=jnp.int32)
    tallies = jnp.zeros((N_ROW, N_ROW, cell_positions), jnp.int32)
    for turn_index in range(STEPS):
        inner_tile = (tile_rows + tile_cols + turn_index) % N_ROW
        a_cells = first_factor_cell_index[tile_rows, inner_tile]
        b_cells = second_factor_cell_index[inner_tile, tile_cols]
        matching = (a_cells % TILE)[:, :, :, None] == (b_cells // TILE)[:, :, None, :]
        product_cell = (a_cells // TILE)[:, :, :, None] * TILE + (b_cells % TILE)[:, :, None, :]
        hits = (product_cell[..., None] == every_cell) & matching[..., None]
        tallies = tallies + jnp.sum(hits.astype(jnp.int32), axis=(2, 3))
    noise = jax.random.randint(jax.random.fold_in(key, 303), (N_ROW, N_ROW, cell_positions), 0, 1 << 20)
    sorted_scores = (tallies > 0).astype(jnp.int32) * (1 << 27) + noise * cell_positions + every_cell[None, None, :]
    c_where = lax.top_k(sorted_scores, SLOTS)[1].astype(jnp.int32)
    return (first_factor_cell_index, second_factor_cell_index, c_where)


def draw_first_factor_cell_index(key, part):
    return pattern_tables(key)[0]


def draw_second_factor_cell_index(key, part):
    return pattern_tables(key)[1]


def draw_c_where(key, part):
    return pattern_tables(key)[2]


def level_of(stream_key, shape, cuts, least, top_value):
    def one(axis_at, parts):
        heights = jax.random.uniform(jax.random.fold_in(jax.random.fold_in(stream_key, 6), axis_at), (parts,), jnp.float32, least / len(cuts), top_value / len(cuts))
        return jnp.repeat(jnp.exp(heights), shape[axis_at] // parts).reshape((-1,) + (1,) * (len(shape) - axis_at - 1))

    level = one(*cuts[0])
    for cut in cuts[1:]:
        level = level * one(*cut)
    return level


def bell_draw(rng, shape, scale, limit, cuts=(), kind=jnp.bfloat16):
    factor_of = level_of(rng, shape, cuts, -0.22, 0.18) if cuts else 1.0
    values = jax.random.normal(rng, shape, jnp.float32) * scale * factor_of
    return jnp.minimum(jnp.maximum(values, -limit), limit).astype(kind)


def setup_inputs(seed: int = 0, part: int = 0) -> dict:
    key_of = jax.random.split(jax.random.key(seed), 6)
    part_splits = jax.random.split(jax.random.fold_in(key_of[5], part), 6)
    return {
        "a_blocks": bell_draw(part_splits[0], (N_COL, N_ROW, SLOTS, BLOCK, BLOCK), BLOCK ** -0.5, 0.3125, ((0, 4), (1, 4)), jnp.float32),
        "first_factor_cell_index": draw_first_factor_cell_index(jax.random.fold_in(jax.random.fold_in(key_of[5], part), 71), part),
        "b_blocks": bell_draw(part_splits[2], (N_COL, N_ROW, SLOTS, BLOCK, BLOCK), 1.0, 6.0, ((0, 4), (1, 4)), jnp.float32),
        "second_factor_cell_index": draw_second_factor_cell_index(jax.random.fold_in(jax.random.fold_in(key_of[5], part), 71), part),
        "c_where": draw_c_where(jax.random.fold_in(jax.random.fold_in(key_of[5], part), 71), part),
    }


def tile_sum(accumulated, a_tile, a_cells, b_tile, b_cells, kept_cells):
    a_blockrow = a_cells // TILE
    a_inner = a_cells % TILE
    b_inner = b_cells // TILE
    b_blockcol = b_cells % TILE
    matching = a_inner[:, None] == b_inner[None, :]
    product_cell = a_blockrow[:, None] * TILE + b_blockcol[None, :]
    weights = (matching[:, :, None] & (product_cell[:, :, None] == kept_cells[None, None, :])).astype(jnp.float32)
    for first in range(a_tile.shape[0]):
        for second in range(b_tile.shape[0]):
            factor = weights[first, second]
            accumulated = lax.cond(
                jnp.any(factor > 0),
                lambda running: running + factor[:, None, None] * jnp.dot(a_tile[first], b_tile[second], precision=lax.Precision.HIGHEST),
                lambda running: running,
                accumulated)
    return accumulated


def reference(a_blocks, first_factor_cell_index, b_blocks, second_factor_cell_index, c_where):
    def one_tile(flat_index):
        row_tile = flat_index // N_ROW
        col_tile = flat_index % N_ROW
        accumulated = jnp.zeros(a_blocks.shape[2:], jnp.float32)
        for turn_index in range(STEPS):
            inner_tile = (row_tile + col_tile + turn_index) % N_ROW
            accumulated = tile_sum(accumulated, a_blocks[row_tile, inner_tile], first_factor_cell_index[row_tile, inner_tile],
                                   b_blocks[inner_tile, col_tile], second_factor_cell_index[inner_tile, col_tile],
                                   c_where[row_tile, col_tile])
        return accumulated
    results = lax.map(one_tile, jnp.arange(N_ROW * N_ROW, dtype=jnp.int32))
    return results.reshape(c_where.shape + a_blocks.shape[3:])
```

```python
import functools

import jax
import jax.numpy as jnp
import numpy as np
from jax import lax
from jax.experimental import pallas as pl
from jax.experimental.pallas import tpu as pltpu
from jax.sharding import PartitionSpec as P

TILE = 7
STEPS = 3
AXES = ("row", "col")

DOWN = (
    [(j, s, s - 1) for j in (0, 1, 3) for s in (1, 2, 3)] + [(2, 2, 0), (2, 3, 2)],
    [(0, 1, 0), (0, 2, 1), (1, 1, 0), (1, 2, 1), (2, 2, 1), (3, 2, 0)],
    [(1, 1, 0), (2, 1, 0)],
)
UP = (
    [(0, 0, 1), (0, 1, 3)] + [(j, s, s + 1) for j in (1, 2, 3) for s in (0, 1, 2)],
    [(0, 1, 2), (1, 1, 2), (1, 2, 3), (2, 1, 2), (2, 2, 3), (3, 1, 3)],
    [(0, 2, 3), (1, 2, 3)],
)


def origins(stages, n):
    held = np.tile(np.arange(n), (n, 1))
    out = []
    for flows in stages:
        got = np.full((n, n), -1)
        for j, source, target in flows:
            got[j, target] = held[j, source]
        held = got
        out.append(got)
    return out


def move(block, flows, n):
    return lax.ppermute(block, AXES, [(j * n + s, j * n + t) for j, s, t in flows])


def multiply(n_first, widths, tile, cells_ref, plan_ref, where_ref, *refs):
    firsts, seconds = refs[:n_first], refs[n_first : n_first + len(widths)]
    out_ref, a_vmem, b_vmem, sems = refs[n_first + len(widths) :]
    out_ref[...] = jnp.zeros_like(out_ref)
    slots = out_ref.shape[0]

    entry = 0
    for second, width in zip(seconds, widths):
        for part in range(width):
            which, a_at, b_at = plan_ref[3 * entry], plan_ref[3 * entry + 1], plan_ref[3 * entry + 2]
            entry += 1

            def one_entry(second=second, part=part, which=which, a_at=a_at, b_at=b_at):
                b_cell = cells_ref[b_at]

                def one_pair(first_slot, carry):
                    a_cell = cells_ref[a_at + first_slot]
                    product = (a_cell // tile) * tile + b_cell % tile
                    matching = a_cell % tile == b_cell // tile
                    kept = [matching & (product == where_ref[c]) for c in range(slots)]

                    @pl.when(functools.reduce(jnp.logical_or, kept))
                    def _():
                        b_copy = pltpu.make_async_copy(second.at[part], b_vmem, sems.at[1])
                        b_copy.start()
                        for m, first in enumerate(firsts):

                            @pl.when(which == m)
                            def _():
                                a_copy = pltpu.make_async_copy(first.at[first_slot], a_vmem, sems.at[0])
                                a_copy.start()
                                a_copy.wait()

                        b_copy.wait()
                        a, b = a_vmem[...], b_vmem[...]
                        a_high = a.astype(jnp.bfloat16)
                        b_high = b.astype(jnp.bfloat16)
                        a_low = (a - a_high.astype(jnp.float32)).astype(jnp.bfloat16)
                        b_low = (b - b_high.astype(jnp.float32)).astype(jnp.bfloat16)
                        dot = functools.partial(jnp.dot, preferred_element_type=jnp.float32)
                        value = dot(a_high, b_high) + (dot(a_high, b_low) + dot(a_low, b_high))
                        for c in range(slots):

                            @pl.when(kept[c])
                            def _():
                                out_ref[c] += value

                    return carry

                lax.fori_loop(0, slots, one_pair, 0)

            pl.when(which >= 0)(one_entry)


def product(cells, plan, where, firsts, seconds):
    slots, rows, columns = firsts[0].shape
    widths = [x.shape[0] for x in seconds]
    smem = pl.BlockSpec(memory_space=pltpu.SMEM)
    return pl.pallas_call(
        functools.partial(multiply, len(firsts), widths, TILE),
        out_shape=jax.ShapeDtypeStruct((slots, rows, columns), jnp.float32),
        in_specs=[smem] * 3 + [pl.BlockSpec(memory_space=pl.ANY)] * (len(firsts) + len(seconds)),
        out_specs=pl.BlockSpec(memory_space=pltpu.VMEM),
        scratch_shapes=[
            pltpu.VMEM((rows, columns), jnp.float32),
            pltpu.VMEM((rows, columns), jnp.float32),
            pltpu.SemaphoreType.DMA((2,)),
        ],
        compiler_params=pltpu.CompilerParams(vmem_limit_bytes=24 * 1024 * 1024),
    )(cells, plan, where, *firsts, *seconds)


def gathered_four(a, b, n):
    a_core = lax.ppermute(a, "row", [(j, j ^ 1) for j in range(n)])
    a_chip = lax.ppermute(a, "row", [(j, j ^ 2) for j in range(n)])
    a_far = lax.ppermute(a_chip, "row", [(j, j ^ 1) for j in range(n)])
    firsts = [a, a_core, a_chip, a_far]
    seconds, tiles = [b], [np.tile(np.arange(n), (n, 1))]
    parts = [b[s : s + 1] for s in range(b.shape[0])]
    down, up = list(parts), list(parts)
    down_tiles, up_tiles = origins(DOWN, n), origins(UP, n)
    got = []
    for stage in range(len(DOWN)):
        for s in range(len(parts)):
            down[s] = move(down[s], DOWN[stage], n)
            up[s] = move(up[s], UP[stage], n)
            got += [(down[s], s, down_tiles[stage]), (up[s], s, up_tiles[stage])]
    entries = [(b, list(range(b.shape[0])), tiles[0])] + [(x, [s], t) for x, s, t in got]
    j, i = np.meshgrid(np.arange(n), np.arange(n), indexing="ij")
    plan = []
    for _, slots, tile in entries:
        inside = (tile >= 0) & ((tile - i - j) % n < STEPS)
        for s in slots:
            plan.append(np.where(inside, tile ^ j, -1))
            plan.append((tile * n + i) * 2 * b.shape[0])
            plan.append((j * n + tile) * 2 * b.shape[0] + b.shape[0] + s)
    return firsts, [x for x, _, _ in entries], np.stack(plan, -1)


def gathered_any(a, b, n):
    firsts, seconds, plan = [], [], []
    j, i = np.meshgrid(np.arange(n), np.arange(n), indexing="ij")
    for step in range(STEPS):
        tile = (i + j + step) % n
        here = (j * n + i).reshape(-1)
        firsts.append(lax.ppermute(a, AXES, list(zip((tile * n + i).reshape(-1).tolist(), here.tolist()))))
        seconds.append(lax.ppermute(b, AXES, list(zip((j * n + tile).reshape(-1).tolist(), here.tolist()))))
        for s in range(b.shape[0]):
            plan.append(np.full((n, n), step))
            plan.append((tile * n + i) * 2 * b.shape[0])
            plan.append((j * n + tile) * 2 * b.shape[0] + b.shape[0] + s)
    return firsts, seconds, np.stack(plan, -1)


def on_device(a_blocks, first_factor_cell_index, b_blocks, second_factor_cell_index, c_where):
    n = lax.axis_size("row")
    own_cells = jnp.concatenate([first_factor_cell_index[0, 0], second_factor_cell_index[0, 0]])
    cells = lax.all_gather(own_cells, AXES).reshape(-1)
    gathered = gathered_four if n == 4 else gathered_any
    firsts, seconds, plan = gathered(a_blocks[0, 0], b_blocks[0, 0], n)
    plan = jnp.asarray(plan, jnp.int32)[lax.axis_index("row"), lax.axis_index("col")]
    return product(cells, plan, c_where[0, 0], firsts, seconds)[None, None]


def solution(mesh):
    return jax.shard_map(
        on_device,
        mesh=mesh,
        in_specs=(
            P(("groups", "col"), "row", None, None, None),
            P(("groups", "col"), "row", None),
            P(("groups", "col"), "row", None, None, None),
            P(("groups", "col"), "row", None),
            P(("groups", "col"), "row", None),
        ),
        out_specs=P(("groups", "col"), "row", None, None, None),
        check_vma=False,
    )
```

```python
import functools

import jax
import jax.numpy as jnp
import numpy as np
from jax import lax
from jax.experimental import pallas as pl
from jax.experimental.pallas import tpu as pltpu
from jax.sharding import PartitionSpec as P

TILE = 7
STEPS = 3
PAD = 8
AXES = ("row", "col")

DOWN = (
    [(j, s, s - 1) for j in (0, 1, 3) for s in (1, 2, 3)] + [(2, 2, 0), (2, 3, 2)],
    [(0, 1, 0), (0, 2, 1), (1, 1, 0), (1, 2, 1), (2, 2, 1), (3, 2, 0)],
    [(1, 1, 0), (2, 1, 0)],
)
UP = (
    [(0, 0, 1), (0, 1, 3)] + [(j, s, s + 1) for j in (1, 2, 3) for s in (0, 1, 2)],
    [(0, 1, 2), (1, 1, 2), (1, 2, 3), (2, 1, 2), (2, 2, 3), (3, 1, 3)],
    [(0, 2, 3), (1, 2, 3)],
)


def origins(stages, n):
    held = np.tile(np.arange(n), (n, 1))
    out = []
    for flows in stages:
        got = np.full((n, n), -1)
        for j, source, target in flows:
            got[j, target] = held[j, source]
        held = got
        out.append(got)
    return out


def move(block, flows, n):
    return lax.ppermute(block, AXES, [(j * n + s, j * n + t) for j, s, t in flows])


def tag_kernel(cell_ref, in_ref, *rest):
    slots, rows, columns = in_ref.shape
    outs, sems = rest[:slots], rest[slots]
    copies = [pltpu.make_async_copy(in_ref.at[s], outs[s].at[pl.ds(0, rows)], sems.at[s]) for s in range(slots)]
    for copy in copies:
        copy.start()
    for s in range(slots):
        outs[s][pl.ds(rows, PAD)] = jnp.full((PAD, columns), cell_ref[s].astype(jnp.float32))
    for copy in copies:
        copy.wait()


def tagged(blocks, cells):
    slots, rows, columns = blocks.shape
    return pl.pallas_call(
        tag_kernel,
        out_shape=[jax.ShapeDtypeStruct((rows + PAD, columns), blocks.dtype)] * slots,
        in_specs=[pl.BlockSpec(memory_space=pltpu.SMEM), pl.BlockSpec(memory_space=pltpu.HBM)],
        out_specs=[pl.BlockSpec(memory_space=pltpu.VMEM)] * slots,
        scratch_shapes=[pltpu.SemaphoreType.DMA((slots,))],
        compiler_params=pltpu.CompilerParams(vmem_limit_bytes=62 * 1024 * 1024),
    )(cells, blocks)


def tag_all_kernel(cell_ref, in_ref, out_ref, sems):
    slots, rows, columns = in_ref.shape
    copy = pltpu.make_async_copy(in_ref, out_ref.at[:, pl.ds(0, rows)], sems.at[0])
    copy.start()
    for s in range(slots):
        out_ref[s, pl.ds(rows, PAD)] = jnp.full((PAD, columns), cell_ref[s].astype(jnp.float32))
    copy.wait()


def tagged_together(blocks, cells):
    slots, rows, columns = blocks.shape
    return pl.pallas_call(
        tag_all_kernel,
        out_shape=jax.ShapeDtypeStruct((slots, rows + PAD, columns), blocks.dtype),
        in_specs=[pl.BlockSpec(memory_space=pltpu.SMEM), pl.BlockSpec(memory_space=pltpu.HBM)],
        out_specs=pl.BlockSpec(memory_space=pltpu.VMEM),
        scratch_shapes=[pltpu.SemaphoreType.DMA((1,))],
        compiler_params=pltpu.CompilerParams(vmem_limit_bytes=62 * 1024 * 1024),
    )(cells, blocks)


def dot_split(a, b):
    a_high, b_high = a.astype(jnp.bfloat16), b.astype(jnp.bfloat16)
    a_low = (a - a_high.astype(jnp.float32)).astype(jnp.bfloat16)
    b_low = (b - b_high.astype(jnp.float32)).astype(jnp.bfloat16)
    dot = functools.partial(jnp.dot, preferred_element_type=jnp.float32)
    return dot(a_high, b_high) + (dot(a_high, b_low) + dot(a_low, b_high))


def kept_cells(a_cell, b_cell, where_ref, slots):
    product = (a_cell // TILE) * TILE + b_cell % TILE
    matching = a_cell % TILE == b_cell // TILE
    return [matching & (product == where_ref[c]) for c in range(slots)]


def multiply(plan_ref, where_ref, *refs, firsts_at, n_arrays, n_second):
    arrays, seconds = refs[:n_arrays], refs[n_arrays : n_arrays + n_second]
    out_ref, a_vmem, b_vmem, a_cells, b_cells, cell_sems, sems = refs[-7:]
    slots, rows, columns = out_ref.shape
    tag = (pl.ds(rows, PAD), pl.ds(0, 128))

    copies = []
    for m, (k, offset) in enumerate(firsts_at):
        for s in range(slots):
            copies.append(pltpu.make_async_copy(arrays[k].at[offset + s, *tag], a_cells.at[m, s], cell_sems.at[0]))
    for e in range(n_second):
        copies.append(pltpu.make_async_copy(seconds[e].at[*tag], b_cells.at[e], cell_sems.at[0]))
    for copy in copies:
        copy.start()
    out_ref[...] = jnp.zeros_like(out_ref)
    for copy in copies:
        copy.wait()

    for entry, second in enumerate(seconds):
        which = plan_ref[entry]

        def one_entry(entry=entry, second=second, which=which):
            b_cell = b_cells[entry, 0, 0].astype(jnp.int32)

            def one_pair(first_slot, carry):
                a_cell = a_cells[which, first_slot, 0, 0].astype(jnp.int32)
                kept = kept_cells(a_cell, b_cell, where_ref, slots)

                @pl.when(functools.reduce(jnp.logical_or, kept))
                def _():
                    b_copy = pltpu.make_async_copy(second.at[pl.ds(0, rows)], b_vmem, sems.at[1])
                    b_copy.start()
                    for m, (k, offset) in enumerate(firsts_at):

                        @pl.when(which == m)
                        def _():
                            source = arrays[k].at[offset + first_slot, pl.ds(0, rows)]
                            a_copy = pltpu.make_async_copy(source, a_vmem, sems.at[0])
                            a_copy.start()
                            a_copy.wait()

                    b_copy.wait()
                    value = dot_split(a_vmem[...], b_vmem[...])
                    for c in range(slots):

                        @pl.when(kept[c])
                        def _():
                            out_ref[c] += value

                return carry

            lax.fori_loop(0, slots, one_pair, 0)

        pl.when(which >= 0)(one_entry)


def multiply_last(plan_ref, where_ref, *refs, firsts_at, n_arrays, n_second):
    for entry in range(n_second):
        last_entry(entry, plan_ref, where_ref, *refs, firsts_at=firsts_at, n_arrays=n_arrays)


def last_entry(entry, plan_ref, where_ref, *refs, firsts_at, n_arrays):
    arrays, second = refs[:n_arrays], refs[n_arrays + entry]
    sums, a_vmem, b_vmem, c_vmem, a_cells, b_cells, cell_sems, sems = refs[-8:]
    slots, rows, columns = sums.shape
    body, tag = pl.ds(0, rows), (pl.ds(rows, PAD), pl.ds(0, 128))
    which = plan_ref[entry]

    @pl.when(which >= 0)
    def _():
        tags = [pltpu.make_async_copy(second.at[*tag], b_cells, cell_sems.at[0])]
        blocks = [pltpu.make_async_copy(second.at[body], b_vmem, sems.at[0])]
        for s in range(slots):
            tags.append(pltpu.make_async_copy(arrays[0].at[s, *tag], a_cells.at[s], cell_sems.at[0]))
            blocks.append(pltpu.make_async_copy(arrays[0].at[s, body], a_vmem.at[s], sems.at[0]))
        blocks.append(pltpu.make_async_copy(sums, c_vmem, sems.at[0]))
        tags[0].start()
        for m, (k, offset) in enumerate(firsts_at):

            @pl.when(which == m)
            def _():
                for s in range(slots):
                    pltpu.make_async_copy(arrays[k].at[offset + s, *tag], a_cells.at[s], cell_sems.at[0]).start()
                for s in range(slots):
                    pltpu.make_async_copy(arrays[k].at[offset + s, body], a_vmem.at[s], sems.at[0]).start()

        blocks[0].start()
        blocks[-1].start()
        for copy in tags + blocks:
            copy.wait()
        b_cell = b_cells[0, 0].astype(jnp.int32)
        for s in range(slots):
            kept = kept_cells(a_cells[s, 0, 0].astype(jnp.int32), b_cell, where_ref, slots)

            @pl.when(functools.reduce(jnp.logical_or, kept))
            def _():
                value = dot_split(a_vmem[s], b_vmem[...])
                for c in range(slots):

                    @pl.when(kept[c])
                    def _():
                        c_vmem[c] += value
                        give = pltpu.make_async_copy(c_vmem.at[c], sums.at[c], sems.at[1])
                        give.start()
                        give.wait()


def add_products(plan, where, firsts, seconds, sums=None):
    slots = where.shape[0]
    rows, columns = seconds[0].shape
    rows -= PAD
    arrays = list({id(x): x for x, _ in firsts}.values())
    firsts_at = [([id(y) for y in arrays].index(id(x)), offset) for x, offset in firsts]
    smem = pl.BlockSpec(memory_space=pltpu.SMEM)
    hbm = pl.BlockSpec(memory_space=pltpu.HBM)
    blocks = [*arrays, *seconds]
    block = pltpu.VMEM((rows, columns), jnp.float32)
    pair = pltpu.VMEM((slots, rows, columns), jnp.float32)
    if sums is None:
        body = functools.partial(multiply, firsts_at=firsts_at, n_arrays=len(arrays), n_second=len(seconds))
        scratch = [block, block, pltpu.SMEM((len(firsts), slots, PAD, 128), jnp.float32)]
        scratch += [pltpu.SMEM((len(seconds), PAD, 128), jnp.float32)]
    else:
        body = functools.partial(multiply_last, firsts_at=firsts_at, n_arrays=len(arrays), n_second=len(seconds))
        scratch = [pair, block, pair, pltpu.SMEM((slots, PAD, 128), jnp.float32), pltpu.SMEM((PAD, 128), jnp.float32)]
        blocks.append(sums)
    return pl.pallas_call(
        body,
        out_shape=jax.ShapeDtypeStruct((slots, rows, columns), jnp.float32),
        in_specs=[smem] * 2 + [hbm] * len(blocks),
        out_specs=pl.BlockSpec(memory_space=pltpu.VMEM) if sums is None else hbm,
        scratch_shapes=scratch + [pltpu.SemaphoreType.DMA((1,)), pltpu.SemaphoreType.DMA((2,))],
        input_output_aliases={} if sums is None else {1 + len(blocks): 0},
        cost_estimate=pl.CostEstimate(
            flops=12 * len(seconds) * rows * columns * columns,
            bytes_accessed=4 * rows * columns * (slots + 2 * len(seconds)),
            transcendentals=0,
        ),
        compiler_params=pltpu.CompilerParams(vmem_limit_bytes=60 * 1024 * 1024),
    )(plan, where, *blocks)


def both_cores(a, a_chip, where, n):
    here = jnp.concatenate([a, a_chip])
    swap = lambda x: lax.ppermute(x, "row", [(p, p ^ 1) for p in range(n)])
    return here, lax.cond(where[0] >= 0, swap, jnp.zeros_like, here)


def by_four(a, a_cells, b, b_cells, where, n):
    parts = list(tagged(b, b_cells))
    slots = range(len(parts))
    j, i = np.meshgrid(np.arange(n), np.arange(n), indexing="ij")
    down_tiles, up_tiles = origins(DOWN, n), origins(UP, n)
    moved = [(part, np.tile(np.arange(n), (n, 1))) for part in parts]
    a, parts[0] = lax.optimization_barrier((a, parts[0]))
    a = tagged_together(a, a_cells)
    a_chip = lax.ppermute(a, "row", [(p, p ^ 2) for p in range(n)])
    down, up = list(parts), list(parts)
    last_tiles = [down_tiles[-1], up_tiles[-1]] * len(parts)
    all_tiles = [t for _, t in moved] + [t for k in range(len(DOWN) - 1) for _ in slots for t in (down_tiles[k], up_tiles[k])]
    plan = [np.where((t >= 0) & ((t - i - j) % n < STEPS), t ^ j, -1) for t in all_tiles + last_tiles]
    n_last = 2
    place = lax.axis_index("row"), lax.axis_index("col")
    plans = [jnp.asarray(np.stack(x, -1), jnp.int32)[place] for x in (plan[:-n_last], plan[-n_last:])]
    for stage in range(len(DOWN) - 1):
        for s in slots:
            if (stage, s) == (1, slots[-1]):
                up[s], plans = lax.optimization_barrier((up[s], plans))
            down[s], up[s] = move(down[s], DOWN[stage], n), move(up[s], UP[stage], n)
            moved += [(down[s], down_tiles[stage]), (up[s], up_tiles[stage])]
    for s in slots:
        down[s], up[s] = move(down[s], DOWN[-1], n), move(up[s], UP[-1], n)
        moved += [(down[s], down_tiles[-1]), (up[s], up_tiles[-1])]
    here, there = both_cores(a, a_chip, where, n)
    firsts = [(here, 0), (there, 0), (here, len(parts)), (there, len(parts))]
    blocks = [x for x, _ in moved]
    sums = add_products(plans[0], where, firsts, blocks[:-n_last])
    return add_products(plans[1], where, firsts, blocks[-n_last:], sums)


def by_any(a, a_cells, b, b_cells, where, n):
    a, parts = tagged_together(a, a_cells), tagged(b, b_cells)
    firsts, seconds, plan = [], [], []
    here = [(j, i) for j in range(n) for i in range(n)]
    for step in range(STEPS):
        from_row = [(((i + j + step) % n) * n + i, j * n + i) for j, i in here]
        from_col = [(j * n + (i + j + step) % n, j * n + i) for j, i in here]
        firsts.append((lax.ppermute(a, AXES, from_row), 0))
        seconds += [lax.ppermute(part, AXES, from_col) for part in parts]
        plan += [step for _ in parts]
    return add_products(jnp.asarray(plan, jnp.int32), where, firsts, seconds)


def on_device(a_blocks, first_factor_cell_index, b_blocks, second_factor_cell_index, c_where):
    n = lax.axis_size("row")
    blocks = (a_blocks, first_factor_cell_index, b_blocks, second_factor_cell_index, c_where)
    return (by_four if n == 4 else by_any)(*(x[0, 0] for x in blocks), n)[None, None]


def solution(mesh):
    return jax.shard_map(
        on_device,
        mesh=mesh,
        in_specs=(
            P(("groups", "col"), "row", None, None, None),
            P(("groups", "col"), "row", None),
            P(("groups", "col"), "row", None, None, None),
            P(("groups", "col"), "row", None),
            P(("groups", "col"), "row", None),
        ),
        out_specs=P(("groups", "col"), "row", None, None, None),
        check_vma=False,
    )
```

```python
import functools

import jax
import jax.numpy as jnp
import numpy as np
from jax import lax
from jax.experimental import pallas as pl
from jax.experimental.pallas import tpu as pltpu
from jax.sharding import PartitionSpec as P

TILE = 7
STEPS = 3
PAD = 8
AXES = ("row", "col")

DOWN = (
    [(j, s, s - 1) for j in (0, 1, 3) for s in (1, 2, 3)] + [(2, 2, 0), (2, 3, 2)],
    [(0, 1, 0), (0, 2, 1), (1, 1, 0), (1, 2, 1), (2, 2, 1), (3, 2, 0)],
    [(1, 1, 0), (2, 1, 0)],
)
UP = (
    [(0, 0, 1), (0, 1, 3)] + [(j, s, s + 1) for j in (1, 2, 3) for s in (0, 1, 2)],
    [(0, 1, 2), (1, 1, 2), (1, 2, 3), (2, 1, 2), (2, 2, 3), (3, 1, 3)],
    [(0, 2, 3), (1, 2, 3)],
)


def origins(stages, n):
    held = np.tile(np.arange(n), (n, 1))
    out = []
    for flows in stages:
        got = np.full((n, n), -1)
        for j, source, target in flows:
            got[j, target] = held[j, source]
        held = got
        out.append(got)
    return out


def move(block, flows, n):
    return lax.ppermute(block, AXES, [(j * n + s, j * n + t) for j, s, t in flows])


def tag_kernel(cells_ref, blocks_ref, *rest, apart):
    slots, rows, columns = blocks_ref.shape
    outs, (cells, sems, cells_sem) = rest[:-3], rest[-3:]
    outs = outs if apart else [outs[0].at[s] for s in range(slots)]
    copies = [pltpu.make_async_copy(blocks_ref.at[s], outs[s].at[pl.ds(0, rows)], sems.at[s]) for s in range(slots)]
    fetch = pltpu.make_async_copy(cells_ref, cells, cells_sem.at[0])
    fetch.start()
    for copy in copies:
        copy.start()
    fetch.wait()
    for s in range(slots):
        outs[s][pl.ds(rows, PAD)] = jnp.full((PAD, columns), cells[s].astype(jnp.float32))
    for copy in copies:
        copy.wait()


def tagged(blocks, cells, apart):
    slots, rows, columns = blocks.shape
    hbm = pl.BlockSpec(memory_space=pltpu.HBM)
    shapes = [(rows + PAD, columns)] * slots if apart else [(slots, rows + PAD, columns)]
    return pl.pallas_call(
        functools.partial(tag_kernel, apart=apart),
        out_shape=[jax.ShapeDtypeStruct(shape, blocks.dtype) for shape in shapes],
        in_specs=[hbm, hbm],
        out_specs=[pl.BlockSpec(memory_space=pltpu.VMEM)] * len(shapes),
        scratch_shapes=[
            pltpu.SMEM((slots,), jnp.int32),
            pltpu.SemaphoreType.DMA((slots,)),
            pltpu.SemaphoreType.DMA((1,)),
        ],
        compiler_params=pltpu.CompilerParams(vmem_limit_bytes=60 * 1024 * 1024),
    )(cells, blocks)


def dot_split(a, b):
    a_high, b_high = a.astype(jnp.bfloat16), b.astype(jnp.bfloat16)
    a_low = (a - a_high.astype(jnp.float32)).astype(jnp.bfloat16)
    b_low = (b - b_high.astype(jnp.float32)).astype(jnp.bfloat16)
    dot = functools.partial(jnp.dot, preferred_element_type=jnp.float32)
    return dot(a_high, b_high) + (dot(a_high, b_low) + dot(a_low, b_high))


def kept_cells(a_cell, b_cell, where_ref, slots):
    product = (a_cell // TILE) * TILE + b_cell % TILE
    matching = a_cell % TILE == b_cell // TILE
    return [matching & (product == where_ref[c]) for c in range(slots)]


def multiply(plan_ref, where_ref, *refs, firsts_at, n_arrays, n_second):
    arrays, seconds = refs[:n_arrays], refs[n_arrays : n_arrays + n_second]
    out_ref, a_vmem, b_vmem, a_cells, b_cells, cell_sems, sems = refs[-7:]
    slots, rows, columns = out_ref.shape
    tag = (pl.ds(rows, PAD), pl.ds(0, 128))

    copies = []
    for m, (k, offset) in enumerate(firsts_at):
        for s in range(slots):
            copies.append(pltpu.make_async_copy(arrays[k].at[offset + s, *tag], a_cells.at[m, s], cell_sems.at[0]))
    for e in range(n_second):
        copies.append(pltpu.make_async_copy(seconds[e].at[*tag], b_cells.at[e], cell_sems.at[0]))
    for copy in copies:
        copy.start()
    out_ref[...] = jnp.zeros_like(out_ref)
    for copy in copies:
        copy.wait()

    for entry, second in enumerate(seconds):
        which = plan_ref[entry]

        def one_entry(entry=entry, second=second, which=which):
            b_cell = b_cells[entry, 0, 0].astype(jnp.int32)

            def one_pair(first_slot, carry):
                a_cell = a_cells[which, first_slot, 0, 0].astype(jnp.int32)
                kept = kept_cells(a_cell, b_cell, where_ref, slots)

                @pl.when(functools.reduce(jnp.logical_or, kept))
                def _():
                    b_copy = pltpu.make_async_copy(second.at[pl.ds(0, rows)], b_vmem, sems.at[1])
                    b_copy.start()
                    for m, (k, offset) in enumerate(firsts_at):

                        @pl.when(which == m)
                        def _():
                            source = arrays[k].at[offset + first_slot, pl.ds(0, rows)]
                            a_copy = pltpu.make_async_copy(source, a_vmem, sems.at[0])
                            a_copy.start()
                            a_copy.wait()

                    b_copy.wait()
                    value = dot_split(a_vmem[...], b_vmem[...])
                    for c in range(slots):

                        @pl.when(kept[c])
                        def _():
                            out_ref[c] += value

                return carry

            lax.fori_loop(0, slots, one_pair, 0)

        pl.when(which >= 0)(one_entry)


def multiply_last(plan_ref, where_ref, *refs, firsts_at, n_arrays, n_second):
    for entry in range(n_second):
        last_entry(entry, plan_ref, where_ref, *refs, firsts_at=firsts_at, n_arrays=n_arrays)


def last_entry(entry, plan_ref, where_ref, *refs, firsts_at, n_arrays):
    arrays, second = refs[:n_arrays], refs[n_arrays + entry]
    sums, a_vmem, b_vmem, c_vmem, a_cells, b_cells, cell_sems, sems = refs[-8:]
    slots, rows, columns = sums.shape
    body, tag = pl.ds(0, rows), (pl.ds(rows, PAD), pl.ds(0, 128))
    which = plan_ref[entry]

    @pl.when(which >= 0)
    def _():
        tags = [pltpu.make_async_copy(second.at[*tag], b_cells, cell_sems.at[0])]
        blocks = [pltpu.make_async_copy(second.at[body], b_vmem, sems.at[0])]
        for s in range(slots):
            tags.append(pltpu.make_async_copy(arrays[0].at[s, *tag], a_cells.at[s], cell_sems.at[0]))
            blocks.append(pltpu.make_async_copy(arrays[0].at[s, body], a_vmem.at[s], sems.at[0]))
        blocks.append(pltpu.make_async_copy(sums, c_vmem, sems.at[0]))
        tags[0].start()
        for m, (k, offset) in enumerate(firsts_at):

            @pl.when(which == m)
            def _():
                for s in range(slots):
                    pltpu.make_async_copy(arrays[k].at[offset + s, *tag], a_cells.at[s], cell_sems.at[0]).start()
                for s in range(slots):
                    pltpu.make_async_copy(arrays[k].at[offset + s, body], a_vmem.at[s], sems.at[0]).start()

        blocks[0].start()
        blocks[-1].start()
        for copy in tags + blocks:
            copy.wait()
        b_cell = b_cells[0, 0].astype(jnp.int32)
        for s in range(slots):
            kept = kept_cells(a_cells[s, 0, 0].astype(jnp.int32), b_cell, where_ref, slots)

            @pl.when(functools.reduce(jnp.logical_or, kept))
            def _():
                value = dot_split(a_vmem[s], b_vmem[...])
                for c in range(slots):

                    @pl.when(kept[c])
                    def _():
                        c_vmem[c] += value
                        give = pltpu.make_async_copy(c_vmem.at[c], sums.at[c], sems.at[1])
                        give.start()
                        give.wait()


def add_products(plan, where, firsts, seconds, sums=None):
    slots = where.shape[0]
    rows, columns = seconds[0].shape
    rows -= PAD
    arrays = list({id(x): x for x, _ in firsts}.values())
    firsts_at = [([id(y) for y in arrays].index(id(x)), offset) for x, offset in firsts]
    smem = pl.BlockSpec(memory_space=pltpu.SMEM)
    hbm = pl.BlockSpec(memory_space=pltpu.HBM)
    blocks = [*arrays, *seconds]
    block = pltpu.VMEM((rows, columns), jnp.float32)
    pair = pltpu.VMEM((slots, rows, columns), jnp.float32)
    if sums is None:
        body = functools.partial(multiply, firsts_at=firsts_at, n_arrays=len(arrays), n_second=len(seconds))
        scratch = [block, block, pltpu.SMEM((len(firsts), slots, PAD, 128), jnp.float32)]
        scratch += [pltpu.SMEM((len(seconds), PAD, 128), jnp.float32)]
    else:
        body = functools.partial(multiply_last, firsts_at=firsts_at, n_arrays=len(arrays), n_second=len(seconds))
        scratch = [pair, block, pair, pltpu.SMEM((slots, PAD, 128), jnp.float32), pltpu.SMEM((PAD, 128), jnp.float32)]
        blocks.append(sums)
    hbm = hbm if sums is None else pl.BlockSpec(memory_space=pl.ANY)
    return pl.pallas_call(
        body,
        out_shape=jax.ShapeDtypeStruct((slots, rows, columns), jnp.float32),
        in_specs=[smem] * 2 + [hbm] * len(blocks),
        out_specs=pl.BlockSpec(memory_space=pltpu.VMEM) if sums is None else hbm,
        scratch_shapes=scratch + [pltpu.SemaphoreType.DMA((1,)), pltpu.SemaphoreType.DMA((2,))],
        input_output_aliases={} if sums is None else {1 + len(blocks): 0},
        cost_estimate=pl.CostEstimate(
            flops=12 * len(seconds) * rows * columns * columns,
            bytes_accessed=4 * rows * columns * (slots + 2 * len(seconds)),
            transcendentals=0,
        ),
        compiler_params=pltpu.CompilerParams(vmem_limit_bytes=(60 if sums is None else 8) * 1024 * 1024),
    )(plan, where, *blocks)


def both_cores(a, a_chip, where, n):
    here = jnp.concatenate([a, a_chip])
    swap = lambda x: lax.ppermute(x, "row", [(p, p ^ 1) for p in range(n)])
    return here, lax.cond(where[0] >= 0, swap, jnp.zeros_like, here)


def by_four(a, a_cells, b, b_cells, where, n):
    parts = list(tagged(b, b_cells, True))
    slots = range(len(parts))
    j, i = np.meshgrid(np.arange(n), np.arange(n), indexing="ij")
    down_tiles, up_tiles = origins(DOWN, n), origins(UP, n)
    moved = [(part, np.tile(np.arange(n), (n, 1))) for part in parts]
    a, parts[0] = lax.optimization_barrier((a, parts[0]))
    (a,) = tagged(a, a_cells, False)
    a_chip = lax.ppermute(a, "row", [(p, p ^ 2) for p in range(n)])
    down, up = list(parts), list(parts)
    last_tiles = [down_tiles[-1], up_tiles[-1]] * len(parts)
    all_tiles = [t for _, t in moved] + [t for k in range(len(DOWN) - 1) for _ in slots for t in (down_tiles[k], up_tiles[k])]
    plan = [np.where((t >= 0) & ((t - i - j) % n < STEPS), t ^ j, -1) for t in all_tiles + last_tiles]
    n_last = 2
    place = lax.axis_index("row"), lax.axis_index("col")
    plans = [jnp.asarray(np.stack(x, -1), jnp.int32)[place] for x in (plan[:-n_last], plan[-n_last:])]
    for stage in range(len(DOWN) - 1):
        for s in slots:
            if (stage, s) == (1, slots[-1]):
                up[s], plans = lax.optimization_barrier((up[s], plans))
            down[s], up[s] = move(down[s], DOWN[stage], n), move(up[s], UP[stage], n)
            moved += [(down[s], down_tiles[stage]), (up[s], up_tiles[stage])]
    for s in slots:
        down[s], up[s] = move(down[s], DOWN[-1], n), move(up[s], UP[-1], n)
        moved += [(down[s], down_tiles[-1]), (up[s], up_tiles[-1])]
    here, there = both_cores(a, a_chip, where, n)
    firsts = [(here, 0), (there, 0), (here, len(parts)), (there, len(parts))]
    blocks = [x for x, _ in moved]
    sums = add_products(plans[0], where, firsts, blocks[:-n_last])
    return add_products(plans[1], where, firsts, blocks[-n_last:], sums)


def by_any(a, a_cells, b, b_cells, where, n):
    (a,), parts = tagged(a, a_cells, False), tagged(b, b_cells, True)
    firsts, seconds, plan = [], [], []
    here = [(j, i) for j in range(n) for i in range(n)]
    for step in range(STEPS):
        from_row = [(((i + j + step) % n) * n + i, j * n + i) for j, i in here]
        from_col = [(j * n + (i + j + step) % n, j * n + i) for j, i in here]
        firsts.append((lax.ppermute(a, AXES, from_row), 0))
        seconds += [lax.ppermute(part, AXES, from_col) for part in parts]
        plan += [step for _ in parts]
    return add_products(jnp.asarray(plan, jnp.int32), where, firsts, seconds)


def on_device(a_blocks, first_factor_cell_index, b_blocks, second_factor_cell_index, c_where):
    n = lax.axis_size("row")
    blocks = (a_blocks, first_factor_cell_index, b_blocks, second_factor_cell_index, c_where)
    return (by_four if n == 4 else by_any)(*(x[0, 0] for x in blocks), n)[None, None]


def solution(mesh):
    return jax.shard_map(
        on_device,
        mesh=mesh,
        in_specs=(
            P(("groups", "col"), "row", None, None, None),
            P(("groups", "col"), "row", None),
            P(("groups", "col"), "row", None, None, None),
            P(("groups", "col"), "row", None),
            P(("groups", "col"), "row", None),
        ),
        out_specs=P(("groups", "col"), "row", None, None, None),
        check_vma=False,
    )
```

```python
import functools

import jax
import jax.numpy as jnp
import numpy as np
from jax import lax
from jax.experimental import pallas as pl
from jax.experimental.pallas import tpu as pltpu
from jax.sharding import PartitionSpec as P

TILE = 7
STEPS = 3
PAD = 8
LANES = 128
LATE = 8
AXES = ("row", "col")

DOWN = (
    [(j, s, s - 1) for j in (0, 1, 3) for s in (1, 2, 3)] + [(2, 2, 0), (2, 3, 2)],
    [(0, 1, 0), (0, 2, 1), (1, 1, 0), (1, 2, 1), (2, 2, 1), (3, 2, 0)],
    [(1, 1, 0), (2, 1, 0)],
)
UP = (
    [(0, 0, 1), (0, 1, 3)] + [(j, s, s + 1) for j in (1, 2, 3) for s in (0, 1, 2)],
    [(0, 1, 2), (1, 1, 2), (1, 2, 3), (2, 1, 2), (2, 2, 3), (3, 1, 3)],
    [(0, 2, 3), (1, 2, 3)],
)


def origins(stages, n):
    held = np.tile(np.arange(n), (n, 1))
    out = []
    for flows in stages:
        got = np.full((n, n), -1)
        for j, source, target in flows:
            got[j, target] = held[j, source]
        held = got
        out.append(got)
    return out


def move(block, flows, n):
    return lax.ppermute(block, AXES, [(j * n + s, j * n + t) for j, s, t in flows])


def tag_kernel(cells_ref, blocks_ref, *rest, apart):
    slots, rows, columns = blocks_ref.shape
    outs, (cells, sems, cells_sem) = rest[:-3], rest[-3:]
    blocks = outs if apart else [outs[0].at[s] for s in range(slots)]
    copies = [pltpu.make_async_copy(blocks_ref.at[s], blocks[s].at[pl.ds(0, rows)], sems.at[s]) for s in range(slots)]
    fetch = pltpu.make_async_copy(cells_ref, cells, cells_sem.at[0])
    fetch.start()
    for copy in copies:
        copy.start()
    fetch.wait()
    group = lax.broadcasted_iota(jnp.int32, (PAD, columns), 1) // LANES
    foot = sum(jnp.where(group == s, cells[s], 0) for s in range(slots)).astype(jnp.float32)
    for block in blocks[:1] if apart else blocks:
        block[pl.ds(rows, PAD)] = foot
    for copy in copies:
        copy.wait()


def tag_twice_kernel(cells_ref, blocks_ref, out_ref, wide_ref, both, cells, sems):
    slots, rows, columns = blocks_ref.shape
    copy = pltpu.make_async_copy(blocks_ref, both.at[:, pl.ds(0, rows)], sems.at[0])
    fetch = pltpu.make_async_copy(cells_ref, cells, sems.at[1])
    fetch.start()
    copy.start()
    fetch.wait()
    group = lax.broadcasted_iota(jnp.int32, (PAD, columns), 1) // LANES
    foot = sum(jnp.where(group == s, cells[s], 0) for s in range(slots)).astype(jnp.float32)
    for s in range(slots):
        both[s, pl.ds(rows, PAD)] = foot
    copy.wait()
    copies = [
        pltpu.make_async_copy(both, out_ref, sems.at[0]),
        pltpu.make_async_copy(both, wide_ref.at[pl.ds(0, slots)], sems.at[1]),
    ]
    for copy in copies:
        copy.start()
    for copy in copies:
        copy.wait()


def tagged_twice(blocks, cells):
    slots, rows, columns = blocks.shape
    hbm = pl.BlockSpec(memory_space=pltpu.HBM)
    shapes = [(slots, rows + PAD, columns), (2 * slots, rows + PAD, columns)]
    return pl.pallas_call(
        tag_twice_kernel,
        out_shape=[jax.ShapeDtypeStruct(shape, blocks.dtype) for shape in shapes],
        in_specs=[hbm, hbm],
        out_specs=[hbm] * 2,
        scratch_shapes=[
            pltpu.VMEM(shapes[0], jnp.float32),
            pltpu.SMEM((slots,), jnp.int32),
            pltpu.SemaphoreType.DMA((2,)),
        ],
        compiler_params=pltpu.CompilerParams(vmem_limit_bytes=60 * 1024 * 1024),
    )(cells, blocks)


def tagged(blocks, cells, apart):
    slots, rows, columns = blocks.shape
    hbm = pl.BlockSpec(memory_space=pltpu.HBM)
    shapes = [(rows + PAD, columns)] + [(rows, columns)] * (slots - 1) if apart else [(slots, rows + PAD, columns)]
    return pl.pallas_call(
        functools.partial(tag_kernel, apart=apart),
        out_shape=[jax.ShapeDtypeStruct(shape, blocks.dtype) for shape in shapes],
        in_specs=[hbm, hbm],
        out_specs=[pl.BlockSpec(memory_space=pltpu.VMEM)] * len(shapes),
        scratch_shapes=[
            pltpu.SMEM((slots,), jnp.int32),
            pltpu.SemaphoreType.DMA((slots,)),
            pltpu.SemaphoreType.DMA((1,)),
        ],
        compiler_params=pltpu.CompilerParams(vmem_limit_bytes=60 * 1024 * 1024),
    )(cells, blocks)


def dot_split(a, b):
    a_high, b_high = a.astype(jnp.bfloat16), b.astype(jnp.bfloat16)
    a_low = (a - a_high.astype(jnp.float32)).astype(jnp.bfloat16)
    b_low = (b - b_high.astype(jnp.float32)).astype(jnp.bfloat16)
    dot = functools.partial(jnp.dot, preferred_element_type=jnp.float32)
    return dot(a_high, b_high) + (dot(a_high, b_low) + dot(a_low, b_high))


def row_and_column(cell):
    row = lax.shift_right_logical(cell * 37, 8)
    return row, cell - row * TILE


def kept_cells(a_place, b_place, where_places):
    (a_row, a_column), (b_row, b_column) = a_place, b_place
    matching = a_column == b_row
    return [matching & (a_row == row) & (b_column == column) for row, column in where_places]


def multiply(plan_hbm, where_hbm, *refs, firsts_at, n_arrays, n_flows, n_late):
    arrays, refs = refs[:n_arrays], refs[n_arrays:]
    out_ref, late_ref, a_vmem, b_vmem, tags, row, cells, hits, plan_ref, where_ref, cell_sems, sems = refs[-12:]
    seconds = refs[:-12]
    slots, rows, columns = out_ref.shape
    body, foot = pl.ds(0, rows), pl.ds(rows, PAD)
    blocks_of = [slots] * (n_flows - n_late) + [1] * n_late
    begins = [sum(blocks_of[:f]) for f in range(n_flows)]

    lanes = pl.ds(0, LANES * slots)
    sources = [arrays[k].at[offset, foot, lanes] for k, offset in firsts_at]
    sources += [seconds[n].at[foot, lanes] for n in begins]
    copies = [pltpu.make_async_copy(x, tags.at[n], cell_sems.at[0]) for n, x in enumerate(sources)]
    copies.append(pltpu.make_async_copy(plan_hbm, plan_ref, cell_sems.at[0]))
    copies.append(pltpu.make_async_copy(where_hbm, where_ref, cell_sems.at[0]))
    for copy in copies:
        copy.start()
    out_ref[...] = jnp.zeros_like(out_ref)
    for copy in copies:
        copy.wait()
    lane = lax.broadcasted_iota(jnp.int32, (PAD, LANES), 1)
    packed = jnp.zeros((PAD, LANES), jnp.float32)
    for n in range(len(sources)):
        for s in range(slots):
            packed = jnp.where(lane == slots * n + s, tags[n, :, pl.ds(LANES * s, LANES)], packed)
    row[...] = packed.astype(jnp.int32)
    copy = pltpu.make_async_copy(row, cells, cell_sems.at[0])
    copy.start()
    copy.wait()

    where_places = [row_and_column(where_ref[c]) for c in range(slots)]
    for n in range(LATE):
        late_ref[n] = 0
    count = jnp.int32(0)
    for f in range(n_flows):
        which = plan_ref[f]
        k = sum(jnp.where(which == m, array, 0) for m, (array, _) in enumerate(firsts_at))
        offset = sum(jnp.where(which == m, offset, 0) for m, (_, offset) in enumerate(firsts_at))
        for s in range(slots):
            b_place = row_and_column(cells[0, slots * (len(firsts_at) + f) + s])
            for first_slot in range(slots):
                a_place = row_and_column(cells[0, slots * jnp.maximum(which, 0) + first_slot])
                kept = [jnp.where(x, 1 << c, 0) for c, x in enumerate(kept_cells(a_place, b_place, where_places))]
                hit = jnp.where(which >= 0, sum(kept), 0)
                here = s < blocks_of[f]

                @pl.when(hit > 0)
                def _(f=f, s=s, k=k, offset=offset, first_slot=first_slot, hit=hit, count=count, here=here):
                    if here:
                        for n, x in enumerate((begins[f] + s, k, offset + first_slot, hit)):
                            hits[4 * count + n] = x
                    else:
                        for n, x in ((0, f - (n_flows - n_late)), (1, k), (2, offset), (3 + first_slot, hit)):
                            late_ref[n] = x

                count = count + jnp.where(hit > 0, int(here), 0)

    def fetch(n, slot):
        entry, k, block = (hits[4 * n + x] for x in range(3))
        for e, second in enumerate(seconds):

            @pl.when(entry == e)
            def _():
                pltpu.make_async_copy(second.at[body], b_vmem.at[slot], sems.at[slot]).start()

        for m, array in enumerate(arrays):

            @pl.when(k == m)
            def _():
                pltpu.make_async_copy(array.at[block, body], a_vmem.at[slot], sems.at[slot]).start()

    @pl.when(count > 0)
    def _():
        fetch(0, 0)

    def one_hit(n, carry):
        slot = n % 2

        @pl.when(n + 1 < count)
        def _():
            fetch(n + 1, 1 - slot)

        pltpu.make_async_copy(seconds[0].at[body], b_vmem.at[slot], sems.at[slot]).wait()
        pltpu.make_async_copy(arrays[0].at[0, body], a_vmem.at[slot], sems.at[slot]).wait()
        value = dot_split(a_vmem[slot], b_vmem[slot])
        for c in range(slots):

            @pl.when((hits[4 * n + 3] >> c) & 1 == 1)
            def _():
                out_ref[c] += value

        return carry

    lax.fori_loop(0, count, one_hit, 0)


def multiply_late(late_ref, *refs, n_arrays, n_second):
    arrays, seconds = refs[:n_arrays], refs[n_arrays : n_arrays + n_second]
    sums, a_vmem, b_vmem, c_vmem, sems = refs[-5:]
    slots = sums.shape[0]
    flow, k, offset = (late_ref[n] for n in range(3))
    hits = [late_ref[3 + s] for s in range(slots)]
    touched = functools.reduce(jnp.bitwise_or, hits)

    @pl.when(touched > 0)
    def _():
        copies = []
        for f, second in enumerate(seconds):
            copies.append((flow == f, pltpu.make_async_copy(second, b_vmem, sems.at[0])))
        for s in range(slots):
            for m, array in enumerate(arrays):
                source = array.at[offset + s, pl.ds(0, a_vmem.shape[1])]
                copies.append(((hits[s] > 0) & (k == m), pltpu.make_async_copy(source, a_vmem.at[s], sems.at[1 + s])))
        takes = [pltpu.make_async_copy(sums.at[c], c_vmem.at[c], sems.at[1 + slots]) for c in range(slots)]
        copies += [((touched >> c) & 1 == 1, take) for c, take in enumerate(takes)]
        for wanted, copy in copies:
            pl.when(wanted)(copy.start)
        for wanted, copy in copies:
            pl.when(wanted)(copy.wait)

        def one_slot(s, carry):
            hit = sum(jnp.where(s == t, hits[t], 0) for t in range(slots))

            @pl.when(hit > 0)
            def _():
                value = dot_split(a_vmem[s], b_vmem[...])
                for c in range(slots):

                    @pl.when((hit >> c) & 1 == 1)
                    def _():
                        c_vmem[c] += value

            return carry

        lax.fori_loop(0, slots, one_slot, 0)
        gives = [pltpu.make_async_copy(c_vmem.at[c], sums.at[c], sems.at[1 + slots]) for c in range(slots)]
        for c, give in enumerate(gives):
            pl.when((touched >> c) & 1 == 1)(give.start)
        for c, give in enumerate(gives):
            pl.when((touched >> c) & 1 == 1)(give.wait)


def arrays_of(firsts):
    arrays = list({id(x): x for x, _ in firsts}.values())
    return arrays, [([id(y) for y in arrays].index(id(x)), offset) for x, offset in firsts]


def add_products(plan, where, firsts, flows, n_late):
    slots, rows, columns = where.shape[0], *flows[0][-1].shape
    arrays, firsts_at = arrays_of(firsts)
    seconds = [x for flow in flows for x in flow]
    smem, hbm = pl.BlockSpec(memory_space=pltpu.SMEM), pl.BlockSpec(memory_space=pltpu.HBM)
    both = pltpu.VMEM((2, rows, columns), jnp.float32)
    return pl.pallas_call(
        functools.partial(
            multiply, firsts_at=firsts_at, n_arrays=len(arrays), n_flows=len(flows), n_late=n_late
        ),
        out_shape=[
            jax.ShapeDtypeStruct((slots, rows, columns), jnp.float32),
            jax.ShapeDtypeStruct((LATE,), jnp.int32),
        ],
        in_specs=[hbm] * (2 + len(arrays) + len(seconds)),
        out_specs=[pl.BlockSpec(memory_space=pltpu.VMEM), smem],
        scratch_shapes=[
            both,
            both,
            pltpu.VMEM((len(firsts) + len(flows), PAD, LANES * slots), jnp.float32),
            pltpu.VMEM((PAD, LANES), jnp.int32),
            pltpu.SMEM((PAD, LANES), jnp.int32),
            pltpu.SMEM((4 * slots * slots * len(flows),), jnp.int32),
            pltpu.SMEM(plan.shape, jnp.int32),
            pltpu.SMEM(where.shape, jnp.int32),
            pltpu.SemaphoreType.DMA((1,)),
            pltpu.SemaphoreType.DMA((2,)),
        ],
        cost_estimate=pl.CostEstimate(
            flops=12 * len(seconds) * rows * columns * columns,
            bytes_accessed=4 * rows * columns * (slots + 2 * len(seconds)),
            transcendentals=0,
        ),
        compiler_params=pltpu.CompilerParams(vmem_limit_bytes=60 * 1024 * 1024),
    )(plan, where, *arrays, *seconds)


def add_late_products(late, firsts, seconds, sums):
    slots, rows, columns = sums.shape
    arrays, _ = arrays_of(firsts)
    where_it_is = pl.BlockSpec(memory_space=pl.ANY)
    blocks = [*arrays, *seconds, sums]
    pair = pltpu.VMEM((slots, rows, columns), jnp.float32)
    return pl.pallas_call(
        functools.partial(multiply_late, n_arrays=len(arrays), n_second=len(seconds)),
        out_shape=jax.ShapeDtypeStruct((slots, rows, columns), jnp.float32),
        in_specs=[pl.BlockSpec(memory_space=pltpu.SMEM)] + [where_it_is] * len(blocks),
        out_specs=where_it_is,
        scratch_shapes=[
            pair,
            pltpu.VMEM((rows, columns), jnp.float32),
            pair,
            pltpu.SemaphoreType.DMA((slots + 2,)),
        ],
        input_output_aliases={len(blocks): 0},
        cost_estimate=pl.CostEstimate(
            flops=12 * len(seconds) * rows * columns * columns,
            bytes_accessed=4 * rows * columns * (slots + 2 * len(seconds)),
            transcendentals=0,
        ),
        compiler_params=pltpu.CompilerParams(vmem_limit_bytes=8 * 1024 * 1024),
    )(late, *blocks)


def both_cores(wide, a_chip, where, n):
    here = lax.dynamic_update_slice(wide, a_chip, (a_chip.shape[0], 0, 0))
    swap = lambda x: lax.ppermute(x, "row", [(p, p ^ 1) for p in range(n)])
    return here, lax.cond(where[0] >= 0, swap, jnp.zeros_like, here)


def by_four(a, a_cells, b, b_cells, where, n):
    parts = list(tagged(b, b_cells, True))
    slots = range(len(parts))
    last = slots[-1]
    j, i = np.meshgrid(np.arange(n), np.arange(n), indexing="ij")
    a, parts[0] = lax.optimization_barrier((a, parts[0]))
    a, wide = tagged_twice(a, a_cells)
    a_chip = lax.ppermute(a, "row", [(p, p ^ 2) for p in range(n)])

    tiles = [np.tile(np.arange(n), (n, 1))]
    for down_tiles, up_tiles in zip(origins(DOWN, n), origins(UP, n)):
        tiles += [down_tiles, up_tiles]
    plan = [np.where((tile >= 0) & ((tile - i - j) % n < STEPS), tile ^ j, -1) for tile in tiles]
    assert not np.any((plan[-2] >= 0) & (plan[-1] >= 0))
    plan = jnp.asarray(np.stack(plan, -1), jnp.int32)[lax.axis_index("row"), lax.axis_index("col")]

    flows = [parts]
    down, up = list(parts), list(parts)
    for stage in range(len(DOWN)):
        for s in slots:
            if (stage, s) == (1, last):
                up[s], plan = lax.optimization_barrier((up[s], plan))
            down[s], up[s] = move(down[s], DOWN[stage], n), move(up[s], UP[stage], n)
        flows += [list(down), list(up)]
    here, there = both_cores(wide, a_chip, where, n)
    firsts = [(here, 0), (there, 0), (here, len(parts)), (there, len(parts))]
    late_blocks = [flow.pop() for flow in flows[-2:]]
    sums, late = add_products(plan, where, firsts, flows, 2)
    return add_late_products(late, firsts, late_blocks, sums)


def by_any(a, a_cells, b, b_cells, where, n):
    (a,), parts = tagged(a, a_cells, False), tagged(b, b_cells, True)
    firsts, flows = [], []
    here = [(j, i) for j in range(n) for i in range(n)]
    for step in range(STEPS):
        from_row = [(((i + j + step) % n) * n + i, j * n + i) for j, i in here]
        from_col = [(j * n + (i + j + step) % n, j * n + i) for j, i in here]
        firsts.append((lax.ppermute(a, AXES, from_row), 0))
        flows.append([lax.ppermute(part, AXES, from_col) for part in parts])
    return add_products(jnp.arange(STEPS, dtype=jnp.int32), where, firsts, flows, 0)[0]


def on_device(a_blocks, first_factor_cell_index, b_blocks, second_factor_cell_index, c_where):
    n = lax.axis_size("row")
    blocks = (a_blocks, first_factor_cell_index, b_blocks, second_factor_cell_index, c_where)
    return (by_four if n == 4 else by_any)(*(x[0, 0] for x in blocks), n)[None, None]


def solution(mesh):
    return jax.shard_map(
        on_device,
        mesh=mesh,
        in_specs=(
            P(("groups", "col"), "row", None, None, None),
            P(("groups", "col"), "row", None),
            P(("groups", "col"), "row", None, None, None),
            P(("groups", "col"), "row", None),
            P(("groups", "col"), "row", None),
        ),
        out_specs=P(("groups", "col"), "row", None, None, None),
        check_vma=False,
    )
```

```python
import functools

import jax
import jax.numpy as jnp
import numpy as np
from jax import lax
from jax.experimental import pallas as pl
from jax.experimental.pallas import tpu as pltpu
from jax.sharding import PartitionSpec as P

TILE = 7
STEPS = 3
PAD = 8
LANES = 128
LATE = 8
AXES = ("row", "col")

DOWN = (
    [(j, s, s - 1) for j in (0, 1, 3) for s in (1, 2, 3)] + [(2, 2, 0), (2, 3, 2)],
    [(0, 1, 0), (0, 2, 1), (1, 1, 0), (1, 2, 1), (2, 2, 1), (3, 2, 0)],
    [(1, 1, 0), (2, 1, 0)],
)
UP = (
    [(0, 0, 1), (0, 1, 3)] + [(j, s, s + 1) for j in (1, 2, 3) for s in (0, 1, 2)],
    [(0, 1, 2), (1, 1, 2), (1, 2, 3), (2, 1, 2), (2, 2, 3), (3, 1, 3)],
    [(0, 2, 3), (1, 2, 3)],
)


def origins(stages, n):
    held = np.tile(np.arange(n), (n, 1))
    out = []
    for flows in stages:
        got = np.full((n, n), -1)
        for j, source, target in flows:
            got[j, target] = held[j, source]
        held = got
        out.append(got)
    return out


def move(block, flows, n):
    return lax.ppermute(block, AXES, [(j * n + s, j * n + t) for j, s, t in flows])


def tag_kernel(cells_ref, blocks_ref, *rest, apart):
    slots, rows, columns = blocks_ref.shape
    outs, (cells, sems, cells_sem) = rest[:-3], rest[-3:]
    blocks = outs if apart else [outs[0].at[s] for s in range(slots)]
    copies = [pltpu.make_async_copy(blocks_ref.at[s], blocks[s].at[pl.ds(0, rows)], sems.at[s]) for s in range(slots)]
    fetch = pltpu.make_async_copy(cells_ref, cells, cells_sem.at[0])
    fetch.start()
    for copy in copies:
        copy.start()
    fetch.wait()
    group = lax.broadcasted_iota(jnp.int32, (PAD, columns), 1) // LANES
    foot = sum(jnp.where(group == s, cells[s], 0) for s in range(slots)).astype(jnp.float32)
    for block in blocks[:1] if apart else blocks:
        block[pl.ds(rows, PAD)] = foot
    for copy in copies:
        copy.wait()


def tag_twice_kernel(cells_ref, blocks_ref, out_ref, wide_ref, both, cells, sems):
    slots, rows, columns = blocks_ref.shape
    copy = pltpu.make_async_copy(blocks_ref, both.at[:, pl.ds(0, rows)], sems.at[0])
    fetch = pltpu.make_async_copy(cells_ref, cells, sems.at[1])
    fetch.start()
    copy.start()
    fetch.wait()
    group = lax.broadcasted_iota(jnp.int32, (PAD, columns), 1) // LANES
    foot = sum(jnp.where(group == s, cells[s], 0) for s in range(slots)).astype(jnp.float32)
    for s in range(slots):
        both[s, pl.ds(rows, PAD)] = foot
    copy.wait()
    copies = [
        pltpu.make_async_copy(both, out_ref, sems.at[0]),
        pltpu.make_async_copy(both, wide_ref.at[pl.ds(0, slots)], sems.at[1]),
    ]
    for copy in copies:
        copy.start()
    for copy in copies:
        copy.wait()


def tagged_twice(blocks, cells):
    slots, rows, columns = blocks.shape
    hbm = pl.BlockSpec(memory_space=pltpu.HBM)
    shapes = [(slots, rows + PAD, columns), (2 * slots, rows + PAD, columns)]
    return pl.pallas_call(
        tag_twice_kernel,
        out_shape=[jax.ShapeDtypeStruct(shape, blocks.dtype) for shape in shapes],
        in_specs=[hbm, hbm],
        out_specs=[hbm] * 2,
        scratch_shapes=[
            pltpu.VMEM(shapes[0], jnp.float32),
            pltpu.SMEM((slots,), jnp.int32),
            pltpu.SemaphoreType.DMA((2,)),
        ],
        compiler_params=pltpu.CompilerParams(vmem_limit_bytes=60 * 1024 * 1024),
    )(cells, blocks)


def tagged(blocks, cells, apart):
    slots, rows, columns = blocks.shape
    hbm = pl.BlockSpec(memory_space=pltpu.HBM)
    shapes = [(rows + PAD, columns)] + [(rows, columns)] * (slots - 1) if apart else [(slots, rows + PAD, columns)]
    return pl.pallas_call(
        functools.partial(tag_kernel, apart=apart),
        out_shape=[jax.ShapeDtypeStruct(shape, blocks.dtype) for shape in shapes],
        in_specs=[hbm, hbm],
        out_specs=[pl.BlockSpec(memory_space=pltpu.VMEM)] * len(shapes),
        scratch_shapes=[
            pltpu.SMEM((slots,), jnp.int32),
            pltpu.SemaphoreType.DMA((slots,)),
            pltpu.SemaphoreType.DMA((1,)),
        ],
        compiler_params=pltpu.CompilerParams(vmem_limit_bytes=60 * 1024 * 1024),
    )(cells, blocks)


def dot_split(a, b):
    a_high, b_high = a.astype(jnp.bfloat16), b.astype(jnp.bfloat16)
    a_low = (a - a_high.astype(jnp.float32)).astype(jnp.bfloat16)
    b_low = (b - b_high.astype(jnp.float32)).astype(jnp.bfloat16)
    dot = functools.partial(jnp.dot, preferred_element_type=jnp.float32)
    return dot(a_high, b_high) + (dot(a_high, b_low) + dot(a_low, b_high))


def row_and_column(cell):
    row = lax.shift_right_logical(cell * 37, 8)
    return row, cell - row * TILE


def kept_cells(a_place, b_place, where_places):
    (a_row, a_column), (b_row, b_column) = a_place, b_place
    matching = a_column == b_row
    return [matching & (a_row == row) & (b_column == column) for row, column in where_places]


def multiply(plan_hbm, where_hbm, *refs, firsts_at, n_arrays, n_flows, n_late):
    arrays, refs = refs[:n_arrays], refs[n_arrays:]
    out_ref, late_ref, a_vmem, b_vmem, tags, row, cells, hits, plan_ref, where_ref, cell_sems, sems = refs[-12:]
    seconds = refs[:-12]
    slots, rows, columns = out_ref.shape
    body, foot = pl.ds(0, rows), pl.ds(rows, PAD)
    blocks_of = [slots] * (n_flows - n_late) + [1] * n_late
    begins = [sum(blocks_of[:f]) for f in range(n_flows)]

    lanes = pl.ds(0, LANES * slots)
    sources = [arrays[k].at[offset, foot, lanes] for k, offset in firsts_at]
    sources += [seconds[n].at[foot, lanes] for n in begins]
    copies = [pltpu.make_async_copy(x, tags.at[n], cell_sems.at[0]) for n, x in enumerate(sources)]
    copies.append(pltpu.make_async_copy(plan_hbm, plan_ref, cell_sems.at[0]))
    copies.append(pltpu.make_async_copy(where_hbm, where_ref, cell_sems.at[0]))
    for copy in copies:
        copy.start()
    out_ref[...] = jnp.zeros_like(out_ref)
    for copy in copies:
        copy.wait()
    lane = lax.broadcasted_iota(jnp.int32, (PAD, LANES), 1)
    packed = jnp.zeros((PAD, LANES), jnp.float32)
    for n in range(len(sources)):
        for s in range(slots):
            packed = jnp.where(lane == slots * n + s, tags[n, :, pl.ds(LANES * s, LANES)], packed)
    row[...] = packed.astype(jnp.int32)
    copy = pltpu.make_async_copy(row, cells, cell_sems.at[0])
    copy.start()
    copy.wait()

    where_places = [row_and_column(where_ref[c]) for c in range(slots)]
    for n in range(LATE):
        late_ref[n] = 0
    count = jnp.int32(0)
    for f in range(n_flows):
        which = plan_ref[f]
        k = sum(jnp.where(which == m, array, 0) for m, (array, _) in enumerate(firsts_at))
        offset = sum(jnp.where(which == m, offset, 0) for m, (_, offset) in enumerate(firsts_at))
        for s in range(slots):
            b_place = row_and_column(cells[0, slots * (len(firsts_at) + f) + s])
            for first_slot in range(slots):
                a_place = row_and_column(cells[0, slots * jnp.maximum(which, 0) + first_slot])
                kept = [jnp.where(x, 1 << c, 0) for c, x in enumerate(kept_cells(a_place, b_place, where_places))]
                hit = jnp.where(which >= 0, sum(kept), 0)
                here = s < blocks_of[f]

                @pl.when(hit > 0)
                def _(f=f, s=s, k=k, offset=offset, first_slot=first_slot, hit=hit, count=count, here=here):
                    if here:
                        for n, x in enumerate((begins[f] + s, k, offset + first_slot, hit)):
                            hits[4 * count + n] = x
                    else:
                        for n, x in ((0, f - (n_flows - n_late)), (1, k), (2, offset), (3 + first_slot, hit)):
                            late_ref[n] = x

                count = count + jnp.where(hit > 0, int(here), 0)

    def fetch(n, slot):
        entry, k, block = (hits[4 * n + x] for x in range(3))
        for e, second in enumerate(seconds):

            @pl.when(entry == e)
            def _():
                pltpu.make_async_copy(second.at[body], b_vmem.at[slot], sems.at[slot]).start()

        for m, array in enumerate(arrays):

            @pl.when(k == m)
            def _():
                pltpu.make_async_copy(array.at[block, body], a_vmem.at[slot], sems.at[slot]).start()

    @pl.when(count > 0)
    def _():
        fetch(0, 0)

    def one_hit(n, carry):
        slot = n % 2

        @pl.when(n + 1 < count)
        def _():
            fetch(n + 1, 1 - slot)

        pltpu.make_async_copy(seconds[0].at[body], b_vmem.at[slot], sems.at[slot]).wait()
        pltpu.make_async_copy(arrays[0].at[0, body], a_vmem.at[slot], sems.at[slot]).wait()
        value = dot_split(a_vmem[slot], b_vmem[slot])
        for c in range(slots):

            @pl.when((hits[4 * n + 3] >> c) & 1 == 1)
            def _():
                out_ref[c] += value

        return carry

    lax.fori_loop(0, count, one_hit, 0)


def multiply_late(late_ref, *refs, n_arrays, n_second):
    arrays, seconds = refs[:n_arrays], refs[n_arrays : n_arrays + n_second]
    sums, a_vmem, b_vmem, c_vmem, sems = refs[-5:]
    slots = sums.shape[0]
    flow, k, offset = (late_ref[n] for n in range(3))
    hits = [late_ref[3 + s] for s in range(slots)]
    touched = functools.reduce(jnp.bitwise_or, hits)

    @pl.when(touched > 0)
    def _():
        copies = []
        for f, second in enumerate(seconds):
            copies.append((flow == f, pltpu.make_async_copy(second, b_vmem, sems.at[0])))
        for s in range(slots):
            for m, array in enumerate(arrays):
                source = array.at[offset + s, pl.ds(0, a_vmem.shape[1])]
                copies.append(((hits[s] > 0) & (k == m), pltpu.make_async_copy(source, a_vmem.at[s], sems.at[1 + s])))
        takes = [pltpu.make_async_copy(sums.at[c], c_vmem.at[c], sems.at[1 + slots]) for c in range(slots)]
        copies += [((touched >> c) & 1 == 1, take) for c, take in enumerate(takes)]
        for wanted, copy in copies:
            pl.when(wanted)(copy.start)
        for wanted, copy in copies:
            pl.when(wanted)(copy.wait)

        def one_slot(s, carry):
            hit = sum(jnp.where(s == t, hits[t], 0) for t in range(slots))

            @pl.when(hit > 0)
            def _():
                value = dot_split(a_vmem[s], b_vmem[...])
                for c in range(slots):

                    @pl.when((hit >> c) & 1 == 1)
                    def _():
                        c_vmem[c] += value

            return carry

        lax.fori_loop(0, slots, one_slot, 0)
        gives = [pltpu.make_async_copy(c_vmem.at[c], sums.at[c], sems.at[1 + slots]) for c in range(slots)]
        for c, give in enumerate(gives):
            pl.when((touched >> c) & 1 == 1)(give.start)
        for c, give in enumerate(gives):
            pl.when((touched >> c) & 1 == 1)(give.wait)


def arrays_of(firsts):
    arrays = list({id(x): x for x, _ in firsts}.values())
    return arrays, [([id(y) for y in arrays].index(id(x)), offset) for x, offset in firsts]


def add_products(plan, where, firsts, flows, n_late):
    slots, rows, columns = where.shape[0], *flows[0][-1].shape
    arrays, firsts_at = arrays_of(firsts)
    seconds = [x for flow in flows for x in flow]
    smem, hbm = pl.BlockSpec(memory_space=pltpu.SMEM), pl.BlockSpec(memory_space=pltpu.HBM)
    both = pltpu.VMEM((2, rows, columns), jnp.float32)
    return pl.pallas_call(
        functools.partial(
            multiply, firsts_at=firsts_at, n_arrays=len(arrays), n_flows=len(flows), n_late=n_late
        ),
        out_shape=[
            jax.ShapeDtypeStruct((slots, rows, columns), jnp.float32),
            jax.ShapeDtypeStruct((LATE,), jnp.int32),
        ],
        in_specs=[hbm] * (2 + len(arrays) + len(seconds)),
        out_specs=[pl.BlockSpec(memory_space=pltpu.VMEM), smem],
        scratch_shapes=[
            both,
            both,
            pltpu.VMEM((len(firsts) + len(flows), PAD, LANES * slots), jnp.float32),
            pltpu.VMEM((PAD, LANES), jnp.int32),
            pltpu.SMEM((PAD, LANES), jnp.int32),
            pltpu.SMEM((4 * slots * slots * len(flows),), jnp.int32),
            pltpu.SMEM(plan.shape, jnp.int32),
            pltpu.SMEM(where.shape, jnp.int32),
            pltpu.SemaphoreType.DMA((1,)),
            pltpu.SemaphoreType.DMA((2,)),
        ],
        cost_estimate=pl.CostEstimate(
            flops=12 * len(seconds) * rows * columns * columns,
            bytes_accessed=4 * rows * columns * (slots + 2 * len(seconds)),
            transcendentals=0,
        ),
        compiler_params=pltpu.CompilerParams(vmem_limit_bytes=53 * 1024 * 1024),
    )(plan, where, *arrays, *seconds)


def add_late_products(late, firsts, seconds, sums):
    slots, rows, columns = sums.shape
    arrays, _ = arrays_of(firsts)
    where_it_is = pl.BlockSpec(memory_space=pl.ANY)
    blocks = [*arrays, *seconds, sums]
    pair = pltpu.VMEM((slots, rows, columns), jnp.float32)
    return pl.pallas_call(
        functools.partial(multiply_late, n_arrays=len(arrays), n_second=len(seconds)),
        out_shape=jax.ShapeDtypeStruct((slots, rows, columns), jnp.float32),
        in_specs=[pl.BlockSpec(memory_space=pltpu.SMEM)] + [where_it_is] * len(blocks),
        out_specs=where_it_is,
        scratch_shapes=[
            pair,
            pltpu.VMEM((rows, columns), jnp.float32),
            pair,
            pltpu.SemaphoreType.DMA((slots + 2,)),
        ],
        input_output_aliases={len(blocks): 0},
        cost_estimate=pl.CostEstimate(
            flops=12 * len(seconds) * rows * columns * columns,
            bytes_accessed=4 * rows * columns * (slots + 2 * len(seconds)),
            transcendentals=0,
        ),
        compiler_params=pltpu.CompilerParams(vmem_limit_bytes=8 * 1024 * 1024),
    )(late, *blocks)


def both_cores(wide, a_chip, where, n):
    here = lax.dynamic_update_slice(wide, a_chip, (a_chip.shape[0], 0, 0))
    swap = lambda x: lax.ppermute(x, "row", [(p, p ^ 1) for p in range(n)])
    return here, lax.cond(where[0] >= 0, swap, jnp.zeros_like, here)


def by_four(a, a_cells, b, b_cells, where, n):
    parts = list(tagged(b, b_cells, True))
    slots = range(len(parts))
    last = slots[-1]
    j, i = np.meshgrid(np.arange(n), np.arange(n), indexing="ij")
    a, parts[0] = lax.optimization_barrier((a, parts[0]))
    a, wide = tagged_twice(a, a_cells)
    a_chip = lax.ppermute(a, "row", [(p, p ^ 2) for p in range(n)])

    tiles = [np.tile(np.arange(n), (n, 1))]
    for down_tiles, up_tiles in zip(origins(DOWN, n), origins(UP, n)):
        tiles += [down_tiles, up_tiles]
    plan = [np.where((tile >= 0) & ((tile - i - j) % n < STEPS), tile ^ j, -1) for tile in tiles]
    assert not np.any((plan[-2] >= 0) & (plan[-1] >= 0))
    plan = jnp.asarray(np.stack(plan, -1), jnp.int32)[lax.axis_index("row"), lax.axis_index("col")]

    flows = [parts]
    down, up = list(parts), list(parts)
    for stage in range(len(DOWN)):
        for s in slots:
            if (stage, s) == (1, last):
                up[s], plan = lax.optimization_barrier((up[s], plan))
            down[s], up[s] = move(down[s], DOWN[stage], n), move(up[s], UP[stage], n)
        flows += [list(down), list(up)]
    here, there = both_cores(wide, a_chip, where, n)
    firsts = [(here, 0), (there, 0), (here, len(parts)), (there, len(parts))]
    late_blocks = [flow.pop() for flow in flows[-2:]]
    sums, late = add_products(plan, where, firsts, flows, 2)
    return add_late_products(late, firsts, late_blocks, sums)


def by_any(a, a_cells, b, b_cells, where, n):
    (a,), parts = tagged(a, a_cells, False), tagged(b, b_cells, True)
    firsts, flows = [], []
    here = [(j, i) for j in range(n) for i in range(n)]
    for step in range(STEPS):
        from_row = [(((i + j + step) % n) * n + i, j * n + i) for j, i in here]
        from_col = [(j * n + (i + j + step) % n, j * n + i) for j, i in here]
        firsts.append((lax.ppermute(a, AXES, from_row), 0))
        flows.append([lax.ppermute(part, AXES, from_col) for part in parts])
    return add_products(jnp.arange(STEPS, dtype=jnp.int32), where, firsts, flows, 0)[0]


def on_device(a_blocks, first_factor_cell_index, b_blocks, second_factor_cell_index, c_where):
    n = lax.axis_size("row")
    blocks = (a_blocks, first_factor_cell_index, b_blocks, second_factor_cell_index, c_where)
    return (by_four if n == 4 else by_any)(*(x[0, 0] for x in blocks), n)[None, None]


def solution(mesh):
    return jax.shard_map(
        on_device,
        mesh=mesh,
        in_specs=(
            P(("groups", "col"), "row", None, None, None),
            P(("groups", "col"), "row", None),
            P(("groups", "col"), "row", None, None, None),
            P(("groups", "col"), "row", None),
            P(("groups", "col"), "row", None),
        ),
        out_specs=P(("groups", "col"), "row", None, None, None),
        check_vma=False,
    )
```

```python
import functools

import jax
import jax.numpy as jnp
import numpy as np
from jax import lax
from jax.experimental import pallas as pl
from jax.experimental.pallas import tpu as pltpu
from jax.sharding import PartitionSpec as P

TILE = 7
STEPS = 3
PAD = 8
LANES = 128
LATE = 8
AXES = ("row", "col")

DOWN = (
    [(j, s, s - 1) for j in (0, 1, 3) for s in (1, 2, 3)] + [(2, 2, 0), (2, 3, 2)],
    [(0, 1, 0), (0, 2, 1), (1, 1, 0), (1, 2, 1), (2, 2, 1), (3, 2, 0)],
    [(1, 1, 0), (2, 1, 0)],
)
UP = (
    [(0, 0, 1), (0, 1, 3)] + [(j, s, s + 1) for j in (1, 2, 3) for s in (0, 1, 2)],
    [(0, 1, 2), (1, 1, 2), (1, 2, 3), (2, 1, 2), (2, 2, 3), (3, 1, 3)],
    [(0, 2, 3), (1, 2, 3)],
)


def origins(stages, n):
    held = np.tile(np.arange(n), (n, 1))
    out = []
    for flows in stages:
        got = np.full((n, n), -1)
        for j, source, target in flows:
            got[j, target] = held[j, source]
        held = got
        out.append(got)
    return out


def move(block, flows, n):
    return lax.ppermute(block, AXES, [(j * n + s, j * n + t) for j, s, t in flows])


def tag_kernel(cells_ref, blocks_ref, *rest, apart):
    slots, rows, columns = blocks_ref.shape
    outs, (cells, sems, cells_sem) = rest[:-3], rest[-3:]
    blocks = outs if apart else [outs[0].at[s] for s in range(slots)]
    copies = [pltpu.make_async_copy(blocks_ref.at[s], blocks[s].at[pl.ds(0, rows)], sems.at[s]) for s in range(slots)]
    fetch = pltpu.make_async_copy(cells_ref, cells, cells_sem.at[0])
    fetch.start()
    for copy in copies:
        copy.start()
    fetch.wait()
    group = lax.broadcasted_iota(jnp.int32, (PAD, columns), 1) // LANES
    foot = sum(jnp.where(group == s, cells[s], 0) for s in range(slots)).astype(jnp.float32)
    for block in blocks[:1] if apart else blocks:
        block[pl.ds(rows, PAD)] = foot
    for copy in copies:
        copy.wait()


def tag_twice_kernel(cells_ref, blocks_ref, out_ref, wide_ref, both, cells, sems):
    slots, rows, columns = blocks_ref.shape
    copy = pltpu.make_async_copy(blocks_ref, both.at[:, pl.ds(0, rows)], sems.at[0])
    fetch = pltpu.make_async_copy(cells_ref, cells, sems.at[1])
    fetch.start()
    copy.start()
    fetch.wait()
    group = lax.broadcasted_iota(jnp.int32, (PAD, columns), 1) // LANES
    foot = sum(jnp.where(group == s, cells[s], 0) for s in range(slots)).astype(jnp.float32)
    for s in range(slots):
        both[s, pl.ds(rows, PAD)] = foot
    copy.wait()
    copies = [
        pltpu.make_async_copy(both, out_ref, sems.at[0]),
        pltpu.make_async_copy(both, wide_ref.at[pl.ds(0, slots)], sems.at[1]),
    ]
    for copy in copies:
        copy.start()
    for copy in copies:
        copy.wait()


def tagged_twice(blocks, cells):
    slots, rows, columns = blocks.shape
    hbm = pl.BlockSpec(memory_space=pltpu.HBM)
    shapes = [(slots, rows + PAD, columns), (2 * slots, rows + PAD, columns)]
    return pl.pallas_call(
        tag_twice_kernel,
        out_shape=[jax.ShapeDtypeStruct(shape, blocks.dtype) for shape in shapes],
        in_specs=[hbm, hbm],
        out_specs=[hbm] * 2,
        scratch_shapes=[
            pltpu.VMEM(shapes[0], jnp.float32),
            pltpu.SMEM((slots,), jnp.int32),
            pltpu.SemaphoreType.DMA((2,)),
        ],
        compiler_params=pltpu.CompilerParams(vmem_limit_bytes=60 * 1024 * 1024),
    )(cells, blocks)


def tagged(blocks, cells, apart):
    slots, rows, columns = blocks.shape
    hbm = pl.BlockSpec(memory_space=pltpu.HBM)
    shapes = [(rows + PAD, columns)] + [(rows, columns)] * (slots - 1) if apart else [(slots, rows + PAD, columns)]
    return pl.pallas_call(
        functools.partial(tag_kernel, apart=apart),
        out_shape=[jax.ShapeDtypeStruct(shape, blocks.dtype) for shape in shapes],
        in_specs=[hbm, hbm],
        out_specs=[pl.BlockSpec(memory_space=pltpu.VMEM)] * len(shapes),
        scratch_shapes=[
            pltpu.SMEM((slots,), jnp.int32),
            pltpu.SemaphoreType.DMA((slots,)),
            pltpu.SemaphoreType.DMA((1,)),
        ],
        compiler_params=pltpu.CompilerParams(vmem_limit_bytes=60 * 1024 * 1024),
    )(cells, blocks)


def dot_split(a, b):
    a_high, b_high = a.astype(jnp.bfloat16), b.astype(jnp.bfloat16)
    a_low = (a - a_high.astype(jnp.float32)).astype(jnp.bfloat16)
    b_low = (b - b_high.astype(jnp.float32)).astype(jnp.bfloat16)
    dot = functools.partial(jnp.dot, preferred_element_type=jnp.float32)
    return dot(a_high, b_high) + (dot(a_high, b_low) + dot(a_low, b_high))


def row_and_column(cell):
    row = lax.shift_right_logical(cell * 37, 8)
    return row, cell - row * TILE


def kept_cells(a_place, b_place, where_places):
    (a_row, a_column), (b_row, b_column) = a_place, b_place
    matching = a_column == b_row
    return [matching & (a_row == row) & (b_column == column) for row, column in where_places]


def multiply(plan_hbm, where_hbm, *refs, firsts_at, n_arrays, n_flows, n_late):
    arrays, refs = refs[:n_arrays], refs[n_arrays:]
    out_hbm, late_ref, out_ref, a_vmem, b_vmem, tags, row, cells, hits, plan_ref, where_ref, cell_sems, sems = refs[-13:]
    seconds = refs[:-13]
    slots, rows, columns = out_ref.shape
    body, foot = pl.ds(0, rows), pl.ds(rows, PAD)
    blocks_of = [slots] * (n_flows - n_late) + [1] * n_late
    begins = [sum(blocks_of[:f]) for f in range(n_flows)]

    lanes = pl.ds(0, LANES * slots)
    sources = [arrays[k].at[offset, foot, lanes] for k, offset in firsts_at]
    sources += [seconds[n].at[foot, lanes] for n in begins]
    copies = [pltpu.make_async_copy(x, tags.at[n], cell_sems.at[0]) for n, x in enumerate(sources)]
    copies.append(pltpu.make_async_copy(plan_hbm, plan_ref, cell_sems.at[0]))
    copies.append(pltpu.make_async_copy(where_hbm, where_ref, cell_sems.at[0]))
    for copy in copies:
        copy.start()
    out_ref[...] = jnp.zeros_like(out_ref)
    for copy in copies:
        copy.wait()
    lane = lax.broadcasted_iota(jnp.int32, (PAD, LANES), 1)
    packed = jnp.zeros((PAD, LANES), jnp.float32)
    for n in range(len(sources)):
        for s in range(slots):
            packed = jnp.where(lane == slots * n + s, tags[n, :, pl.ds(LANES * s, LANES)], packed)
    row[...] = packed.astype(jnp.int32)
    copy = pltpu.make_async_copy(row, cells, cell_sems.at[0])
    copy.start()
    copy.wait()

    where_places = [row_and_column(where_ref[c]) for c in range(slots)]
    for n in range(LATE):
        late_ref[n] = 0
    count, touched = jnp.int32(0), jnp.int32(0)
    for f in range(n_flows):
        which = plan_ref[f]
        k = sum(jnp.where(which == m, array, 0) for m, (array, _) in enumerate(firsts_at))
        offset = sum(jnp.where(which == m, offset, 0) for m, (_, offset) in enumerate(firsts_at))
        for s in range(slots):
            b_place = row_and_column(cells[0, slots * (len(firsts_at) + f) + s])
            for first_slot in range(slots):
                a_place = row_and_column(cells[0, slots * jnp.maximum(which, 0) + first_slot])
                kept = [jnp.where(x, 1 << c, 0) for c, x in enumerate(kept_cells(a_place, b_place, where_places))]
                hit = jnp.where(which >= 0, sum(kept), 0)
                here = s < blocks_of[f]

                @pl.when(hit > 0)
                def _(f=f, s=s, k=k, offset=offset, first_slot=first_slot, hit=hit, count=count, here=here):
                    if here:
                        for n, x in enumerate((begins[f] + s, k, offset + first_slot, hit)):
                            hits[4 * count + n] = x
                    else:
                        for n, x in ((0, f - (n_flows - n_late)), (1, k), (2, offset), (3 + first_slot, hit)):
                            late_ref[n] = x

                count = count + jnp.where(hit > 0, int(here), 0)
                touched = touched | (hit if here else 0)

    gives = [pltpu.make_async_copy(out_ref.at[c], out_hbm.at[c], cell_sems.at[0]) for c in range(slots)]
    for c, give in enumerate(gives):
        pl.when((touched >> c) & 1 == 0)(give.start)

    def fetch(n, slot):
        entry, k, block = (hits[4 * n + x] for x in range(3))
        for e, second in enumerate(seconds):

            @pl.when(entry == e)
            def _():
                pltpu.make_async_copy(second.at[body], b_vmem.at[slot], sems.at[slot]).start()

        for m, array in enumerate(arrays):

            @pl.when(k == m)
            def _():
                pltpu.make_async_copy(array.at[block, body], a_vmem.at[slot], sems.at[slot]).start()

    @pl.when(count > 0)
    def _():
        fetch(0, 0)

    def one_hit(n, carry):
        slot = n % 2

        @pl.when(n + 1 < count)
        def _():
            fetch(n + 1, 1 - slot)

        pltpu.make_async_copy(seconds[0].at[body], b_vmem.at[slot], sems.at[slot]).wait()
        pltpu.make_async_copy(arrays[0].at[0, body], a_vmem.at[slot], sems.at[slot]).wait()
        value = dot_split(a_vmem[slot], b_vmem[slot])
        for c in range(slots):

            @pl.when((hits[4 * n + 3] >> c) & 1 == 1)
            def _():
                out_ref[c] += value

        return carry

    lax.fori_loop(0, count, one_hit, 0)
    for c, give in enumerate(gives):
        pl.when((touched >> c) & 1 == 1)(give.start)
    for give in gives:
        give.wait()


def multiply_late(late_ref, *refs, n_arrays, n_second):
    arrays, seconds = refs[:n_arrays], refs[n_arrays : n_arrays + n_second]
    sums, a_vmem, b_vmem, c_vmem, sems = refs[-5:]
    slots = sums.shape[0]
    flow, k, offset = (late_ref[n] for n in range(3))
    hits = [late_ref[3 + s] for s in range(slots)]
    touched = functools.reduce(jnp.bitwise_or, hits)

    @pl.when(touched > 0)
    def _():
        copies = []
        for f, second in enumerate(seconds):
            copies.append((flow == f, pltpu.make_async_copy(second, b_vmem, sems.at[0])))
        for s in range(slots):
            for m, array in enumerate(arrays):
                source = array.at[offset + s, pl.ds(0, a_vmem.shape[1])]
                copies.append(((hits[s] > 0) & (k == m), pltpu.make_async_copy(source, a_vmem.at[s], sems.at[1 + s])))
        takes = [pltpu.make_async_copy(sums.at[c], c_vmem.at[c], sems.at[1 + slots]) for c in range(slots)]
        copies += [((touched >> c) & 1 == 1, take) for c, take in enumerate(takes)]
        for wanted, copy in copies:
            pl.when(wanted)(copy.start)
        for wanted, copy in copies:
            pl.when(wanted)(copy.wait)

        def one_slot(s, carry):
            hit = sum(jnp.where(s == t, hits[t], 0) for t in range(slots))

            @pl.when(hit > 0)
            def _():
                value = dot_split(a_vmem[s], b_vmem[...])
                for c in range(slots):

                    @pl.when((hit >> c) & 1 == 1)
                    def _():
                        c_vmem[c] += value

            return carry

        lax.fori_loop(0, slots, one_slot, 0)
        gives = [pltpu.make_async_copy(c_vmem.at[c], sums.at[c], sems.at[1 + slots]) for c in range(slots)]
        for c, give in enumerate(gives):
            pl.when((touched >> c) & 1 == 1)(give.start)
        for c, give in enumerate(gives):
            pl.when((touched >> c) & 1 == 1)(give.wait)


def arrays_of(firsts):
    arrays = list({id(x): x for x, _ in firsts}.values())
    return arrays, [([id(y) for y in arrays].index(id(x)), offset) for x, offset in firsts]


def add_products(plan, where, firsts, flows, n_late):
    slots, rows, columns = where.shape[0], *flows[0][-1].shape
    arrays, firsts_at = arrays_of(firsts)
    seconds = [x for flow in flows for x in flow]
    smem, hbm = pl.BlockSpec(memory_space=pltpu.SMEM), pl.BlockSpec(memory_space=pltpu.HBM)
    both = pltpu.VMEM((2, rows, columns), jnp.float32)
    return pl.pallas_call(
        functools.partial(
            multiply, firsts_at=firsts_at, n_arrays=len(arrays), n_flows=len(flows), n_late=n_late
        ),
        out_shape=[
            jax.ShapeDtypeStruct((slots, rows, columns), jnp.float32),
            jax.ShapeDtypeStruct((LATE,), jnp.int32),
        ],
        in_specs=[hbm] * (2 + len(arrays) + len(seconds)),
        out_specs=[hbm, smem],
        scratch_shapes=[
            pltpu.VMEM((slots, rows, columns), jnp.float32),
            both,
            both,
            pltpu.VMEM((len(firsts) + len(flows), PAD, LANES * slots), jnp.float32),
            pltpu.VMEM((PAD, LANES), jnp.int32),
            pltpu.SMEM((PAD, LANES), jnp.int32),
            pltpu.SMEM((4 * slots * slots * len(flows),), jnp.int32),
            pltpu.SMEM(plan.shape, jnp.int32),
            pltpu.SMEM(where.shape, jnp.int32),
            pltpu.SemaphoreType.DMA((1,)),
            pltpu.SemaphoreType.DMA((2,)),
        ],
        cost_estimate=pl.CostEstimate(
            flops=12 * len(seconds) * rows * columns * columns,
            bytes_accessed=4 * rows * columns * (slots + 2 * len(seconds)),
            transcendentals=0,
        ),
        compiler_params=pltpu.CompilerParams(vmem_limit_bytes=60 * 1024 * 1024),
    )(plan, where, *arrays, *seconds)


def add_late_products(late, firsts, seconds, sums):
    slots, rows, columns = sums.shape
    arrays, _ = arrays_of(firsts)
    where_it_is = pl.BlockSpec(memory_space=pl.ANY)
    blocks = [*arrays, *seconds, sums]
    pair = pltpu.VMEM((slots, rows, columns), jnp.float32)
    return pl.pallas_call(
        functools.partial(multiply_late, n_arrays=len(arrays), n_second=len(seconds)),
        out_shape=jax.ShapeDtypeStruct((slots, rows, columns), jnp.float32),
        in_specs=[pl.BlockSpec(memory_space=pltpu.SMEM)] + [where_it_is] * len(blocks),
        out_specs=where_it_is,
        scratch_shapes=[
            pair,
            pltpu.VMEM((rows, columns), jnp.float32),
            pair,
            pltpu.SemaphoreType.DMA((slots + 2,)),
        ],
        input_output_aliases={len(blocks): 0},
        cost_estimate=pl.CostEstimate(
            flops=12 * len(seconds) * rows * columns * columns,
            bytes_accessed=4 * rows * columns * (slots + 2 * len(seconds)),
            transcendentals=0,
        ),
        compiler_params=pltpu.CompilerParams(vmem_limit_bytes=8 * 1024 * 1024),
    )(late, *blocks)


def both_cores(wide, a_chip, where, n):
    here = lax.dynamic_update_slice(wide, a_chip, (a_chip.shape[0], 0, 0))
    swap = lambda x: lax.ppermute(x, "row", [(p, p ^ 1) for p in range(n)])
    return here, lax.cond(where[0] >= 0, swap, jnp.zeros_like, here)


def by_four(a, a_cells, b, b_cells, where, n):
    parts = list(tagged(b, b_cells, True))
    slots = range(len(parts))
    last = slots[-1]
    j, i = np.meshgrid(np.arange(n), np.arange(n), indexing="ij")
    a, parts[0] = lax.optimization_barrier((a, parts[0]))
    a, wide = tagged_twice(a, a_cells)
    a_chip = lax.ppermute(a, "row", [(p, p ^ 2) for p in range(n)])

    tiles = [np.tile(np.arange(n), (n, 1))]
    for down_tiles, up_tiles in zip(origins(DOWN, n), origins(UP, n)):
        tiles += [down_tiles, up_tiles]
    plan = [np.where((tile >= 0) & ((tile - i - j) % n < STEPS), tile ^ j, -1) for tile in tiles]
    assert not np.any((plan[-2] >= 0) & (plan[-1] >= 0))
    plan = jnp.asarray(np.stack(plan, -1), jnp.int32)[lax.axis_index("row"), lax.axis_index("col")]

    flows = [parts]
    down, up = list(parts), list(parts)
    for stage in range(len(DOWN)):
        for s in slots:
            if (stage, s) == (1, last):
                up[s], plan = lax.optimization_barrier((up[s], plan))
            down[s], up[s] = move(down[s], DOWN[stage], n), move(up[s], UP[stage], n)
        flows += [list(down), list(up)]
    here, there = both_cores(wide, a_chip, where, n)
    firsts = [(here, 0), (there, 0), (here, len(parts)), (there, len(parts))]
    late_blocks = [flow.pop() for flow in flows[-2:]]
    sums, late = add_products(plan, where, firsts, flows, 2)
    return add_late_products(late, firsts, late_blocks, sums)


def by_any(a, a_cells, b, b_cells, where, n):
    (a,), parts = tagged(a, a_cells, False), tagged(b, b_cells, True)
    firsts, flows = [], []
    here = [(j, i) for j in range(n) for i in range(n)]
    for step in range(STEPS):
        from_row = [(((i + j + step) % n) * n + i, j * n + i) for j, i in here]
        from_col = [(j * n + (i + j + step) % n, j * n + i) for j, i in here]
        firsts.append((lax.ppermute(a, AXES, from_row), 0))
        flows.append([lax.ppermute(part, AXES, from_col) for part in parts])
    return add_products(jnp.arange(STEPS, dtype=jnp.int32), where, firsts, flows, 0)[0]


def on_device(a_blocks, first_factor_cell_index, b_blocks, second_factor_cell_index, c_where):
    n = lax.axis_size("row")
    blocks = (a_blocks, first_factor_cell_index, b_blocks, second_factor_cell_index, c_where)
    return (by_four if n == 4 else by_any)(*(x[0, 0] for x in blocks), n)[None, None]


def solution(mesh):
    return jax.shard_map(
        on_device,
        mesh=mesh,
        in_specs=(
            P(("groups", "col"), "row", None, None, None),
            P(("groups", "col"), "row", None),
            P(("groups", "col"), "row", None, None, None),
            P(("groups", "col"), "row", None),
            P(("groups", "col"), "row", None),
        ),
        out_specs=P(("groups", "col"), "row", None, None, None),
        check_vma=False,
    )
```

```python
import functools

import jax
import jax.numpy as jnp
import numpy as np
from jax import lax
from jax.experimental import pallas as pl
from jax.experimental.pallas import tpu as pltpu
from jax.sharding import PartitionSpec as P

TILE = 7
STEPS = 3
PAD = 8
LANES = 128
LATE = 8
AXES = ("row", "col")

DOWN = (
    [(j, s, s - 1) for j in (0, 1, 3) for s in (1, 2, 3)] + [(2, 2, 0), (2, 3, 2)],
    [(0, 1, 0), (0, 2, 1), (1, 1, 0), (1, 2, 1), (2, 2, 1), (3, 2, 0)],
    [(1, 1, 0), (2, 1, 0)],
)
UP = (
    [(0, 0, 1), (0, 1, 3)] + [(j, s, s + 1) for j in (1, 2, 3) for s in (0, 1, 2)],
    [(0, 1, 2), (1, 1, 2), (1, 2, 3), (2, 1, 2), (2, 2, 3), (3, 1, 3)],
    [(0, 2, 3), (1, 2, 3)],
)


def origins(stages, n):
    held = np.tile(np.arange(n), (n, 1))
    out = []
    for flows in stages:
        got = np.full((n, n), -1)
        for j, source, target in flows:
            got[j, target] = held[j, source]
        held = got
        out.append(got)
    return out


def move(block, flows, n):
    return lax.ppermute(block, AXES, [(j * n + s, j * n + t) for j, s, t in flows])


def tag_kernel(cells_ref, blocks_ref, *rest, apart):
    slots, rows, columns = blocks_ref.shape
    outs, (cells, sems, cells_sem) = rest[:-3], rest[-3:]
    blocks = outs if apart else [outs[0].at[s] for s in range(slots)]
    copies = [pltpu.make_async_copy(blocks_ref.at[s], blocks[s].at[pl.ds(0, rows)], sems.at[s]) for s in range(slots)]
    fetch = pltpu.make_async_copy(cells_ref, cells, cells_sem.at[0])
    fetch.start()
    for copy in copies:
        copy.start()
    fetch.wait()
    group = lax.broadcasted_iota(jnp.int32, (PAD, columns), 1) // LANES
    foot = sum(jnp.where(group == s, cells[s], 0) for s in range(slots)).astype(jnp.float32)
    for block in blocks[:1] if apart else blocks:
        block[pl.ds(rows, PAD)] = foot
    for copy in copies:
        copy.wait()


def tag_twice_kernel(cells_ref, blocks_ref, out_ref, wide_ref, both, cells, sems):
    slots, rows, columns = blocks_ref.shape
    copy = pltpu.make_async_copy(blocks_ref, both.at[:, pl.ds(0, rows)], sems.at[0])
    fetch = pltpu.make_async_copy(cells_ref, cells, sems.at[1])
    fetch.start()
    copy.start()
    fetch.wait()
    group = lax.broadcasted_iota(jnp.int32, (PAD, columns), 1) // LANES
    foot = sum(jnp.where(group == s, cells[s], 0) for s in range(slots)).astype(jnp.float32)
    for s in range(slots):
        both[s, pl.ds(rows, PAD)] = foot
    copy.wait()
    copies = [
        pltpu.make_async_copy(both, out_ref, sems.at[0]),
        pltpu.make_async_copy(both, wide_ref.at[pl.ds(0, slots)], sems.at[1]),
    ]
    for copy in copies:
        copy.start()
    for copy in copies:
        copy.wait()


def tagged_twice(blocks, cells):
    slots, rows, columns = blocks.shape
    hbm = pl.BlockSpec(memory_space=pltpu.HBM)
    shapes = [(slots, rows + PAD, columns), (2 * slots, rows + PAD, columns)]
    return pl.pallas_call(
        tag_twice_kernel,
        out_shape=[jax.ShapeDtypeStruct(shape, blocks.dtype) for shape in shapes],
        in_specs=[hbm, hbm],
        out_specs=[hbm] * 2,
        scratch_shapes=[
            pltpu.VMEM(shapes[0], jnp.float32),
            pltpu.SMEM((slots,), jnp.int32),
            pltpu.SemaphoreType.DMA((2,)),
        ],
        compiler_params=pltpu.CompilerParams(vmem_limit_bytes=60 * 1024 * 1024),
    )(cells, blocks)


def tagged(blocks, cells, apart):
    slots, rows, columns = blocks.shape
    hbm = pl.BlockSpec(memory_space=pltpu.HBM)
    shapes = [(rows + PAD, columns)] + [(rows, columns)] * (slots - 1) if apart else [(slots, rows + PAD, columns)]
    return pl.pallas_call(
        functools.partial(tag_kernel, apart=apart),
        out_shape=[jax.ShapeDtypeStruct(shape, blocks.dtype) for shape in shapes],
        in_specs=[hbm, hbm],
        out_specs=[pl.BlockSpec(memory_space=pltpu.VMEM)] * len(shapes),
        scratch_shapes=[
            pltpu.SMEM((slots,), jnp.int32),
            pltpu.SemaphoreType.DMA((slots,)),
            pltpu.SemaphoreType.DMA((1,)),
        ],
        compiler_params=pltpu.CompilerParams(vmem_limit_bytes=60 * 1024 * 1024),
    )(cells, blocks)


def dot_split(a, b):
    a_high, b_high = a.astype(jnp.bfloat16), b.astype(jnp.bfloat16)
    a_low = (a - a_high.astype(jnp.float32)).astype(jnp.bfloat16)
    b_low = (b - b_high.astype(jnp.float32)).astype(jnp.bfloat16)
    dot = functools.partial(jnp.dot, preferred_element_type=jnp.float32)
    return dot(a_high, b_high) + (dot(a_high, b_low) + dot(a_low, b_high))


def row_and_column(cell):
    row = lax.shift_right_logical(cell * 37, 8)
    return row, cell - row * TILE


def kept_cells(a_place, b_place, where_places):
    (a_row, a_column), (b_row, b_column) = a_place, b_place
    matching = a_column == b_row
    return [matching & (a_row == row) & (b_column == column) for row, column in where_places]


def multiply(plan_hbm, where_hbm, *refs, firsts_at, n_arrays, n_flows, n_late):
    arrays, refs = refs[:n_arrays], refs[n_arrays:]
    out_ref, late_ref, a_vmem, b_vmem, tags, row, cells, hits, plan_ref, where_ref, cell_sems, sems = refs[-12:]
    seconds = refs[:-12]
    slots, rows, columns = out_ref.shape
    body, foot = pl.ds(0, rows), pl.ds(rows, PAD)
    blocks_of = [slots] * (n_flows - n_late) + [1] * n_late
    begins = [sum(blocks_of[:f]) for f in range(n_flows)]

    lanes = pl.ds(0, LANES * slots)
    sources = [arrays[k].at[offset, foot, lanes] for k, offset in firsts_at]
    sources += [seconds[n].at[foot, lanes] for n in begins]
    copies = [pltpu.make_async_copy(x, tags.at[n], cell_sems.at[0]) for n, x in enumerate(sources)]
    copies.append(pltpu.make_async_copy(plan_hbm, plan_ref, cell_sems.at[0]))
    copies.append(pltpu.make_async_copy(where_hbm, where_ref, cell_sems.at[0]))
    for copy in copies:
        copy.start()
    out_ref[...] = jnp.zeros_like(out_ref)
    for copy in copies:
        copy.wait()
    lane = lax.broadcasted_iota(jnp.int32, (PAD, LANES), 1)
    packed = jnp.zeros((PAD, LANES), jnp.float32)
    for n in range(len(sources)):
        for s in range(slots):
            packed = jnp.where(lane == slots * n + s, tags[n, :, pl.ds(LANES * s, LANES)], packed)
    row[...] = packed.astype(jnp.int32)
    copy = pltpu.make_async_copy(row, cells, cell_sems.at[0])
    copy.start()
    copy.wait()

    where_places = [row_and_column(where_ref[c]) for c in range(slots)]
    for n in range(LATE):
        late_ref[n] = 0
    count = jnp.int32(0)
    for f in range(n_flows):
        which = plan_ref[f]
        k = sum(jnp.where(which == m, array, 0) for m, (array, _) in enumerate(firsts_at))
        offset = sum(jnp.where(which == m, offset, 0) for m, (_, offset) in enumerate(firsts_at))
        for s in range(slots):
            b_place = row_and_column(cells[0, slots * (len(firsts_at) + f) + s])
            for first_slot in range(slots):
                a_place = row_and_column(cells[0, slots * jnp.maximum(which, 0) + first_slot])
                kept = [jnp.where(x, 1 << c, 0) for c, x in enumerate(kept_cells(a_place, b_place, where_places))]
                hit = jnp.where(which >= 0, sum(kept), 0)
                here = s < blocks_of[f]

                @pl.when(hit > 0)
                def _(f=f, s=s, k=k, offset=offset, first_slot=first_slot, hit=hit, count=count, here=here):
                    if here:
                        for n, x in enumerate((begins[f] + s, k, offset + first_slot, hit)):
                            hits[4 * count + n] = x
                    else:
                        for n, x in ((0, f - (n_flows - n_late)), (1, k), (2, offset), (3 + first_slot, hit)):
                            late_ref[n] = x

                count = count + jnp.where(hit > 0, int(here), 0)

    def fetch(n, slot):
        entry, k, block = (hits[4 * n + x] for x in range(3))
        for e, second in enumerate(seconds):

            @pl.when(entry == e)
            def _():
                pltpu.make_async_copy(second.at[body], b_vmem.at[slot], sems.at[slot]).start()

        for m, array in enumerate(arrays):

            @pl.when(k == m)
            def _():
                pltpu.make_async_copy(array.at[block, body], a_vmem.at[slot], sems.at[slot]).start()

    @pl.when(count > 0)
    def _():
        fetch(0, 0)

    def one_hit(n, carry):
        slot = n % 2

        @pl.when(n + 1 < count)
        def _():
            fetch(n + 1, 1 - slot)

        pltpu.make_async_copy(seconds[0].at[body], b_vmem.at[slot], sems.at[slot]).wait()
        pltpu.make_async_copy(arrays[0].at[0, body], a_vmem.at[slot], sems.at[slot]).wait()
        value = dot_split(a_vmem[slot], b_vmem[slot])
        for c in range(slots):

            @pl.when((hits[4 * n + 3] >> c) & 1 == 1)
            def _():
                out_ref[c] += value

        return carry

    lax.fori_loop(0, count, one_hit, 0)


def multiply_late(late_hbm, *refs, n_arrays, n_second):
    arrays, seconds = refs[:n_arrays], refs[n_arrays : n_arrays + n_second]
    sums, a_vmem, b_vmem, c_vmem, late_ref, sems = refs[-6:]
    slots = sums.shape[0]
    fetch = pltpu.make_async_copy(late_hbm, late_ref, sems.at[0])
    fetch.start()
    fetch.wait()
    flow, k, offset = (late_ref[n] for n in range(3))
    hits = [late_ref[3 + s] for s in range(slots)]
    touched = functools.reduce(jnp.bitwise_or, hits)

    @pl.when(touched > 0)
    def _():
        copies = []
        for f, second in enumerate(seconds):
            copies.append((flow == f, pltpu.make_async_copy(second, b_vmem, sems.at[0])))
        for s in range(slots):
            for m, array in enumerate(arrays):
                source = array.at[offset + s, pl.ds(0, a_vmem.shape[1])]
                copies.append(((hits[s] > 0) & (k == m), pltpu.make_async_copy(source, a_vmem.at[s], sems.at[1 + s])))
        takes = [pltpu.make_async_copy(sums.at[c], c_vmem.at[c], sems.at[1 + slots]) for c in range(slots)]
        copies += [((touched >> c) & 1 == 1, take) for c, take in enumerate(takes)]
        for wanted, copy in copies:
            pl.when(wanted)(copy.start)
        for wanted, copy in copies:
            pl.when(wanted)(copy.wait)

        def one_slot(s, carry):
            hit = sum(jnp.where(s == t, hits[t], 0) for t in range(slots))

            @pl.when(hit > 0)
            def _():
                value = dot_split(a_vmem[s], b_vmem[...])
                for c in range(slots):

                    @pl.when((hit >> c) & 1 == 1)
                    def _():
                        c_vmem[c] += value

            return carry

        lax.fori_loop(0, slots, one_slot, 0)
        gives = [pltpu.make_async_copy(c_vmem.at[c], sums.at[c], sems.at[1 + slots]) for c in range(slots)]
        for c, give in enumerate(gives):
            pl.when((touched >> c) & 1 == 1)(give.start)
        for c, give in enumerate(gives):
            pl.when((touched >> c) & 1 == 1)(give.wait)


def arrays_of(firsts):
    arrays = list({id(x): x for x, _ in firsts}.values())
    return arrays, [([id(y) for y in arrays].index(id(x)), offset) for x, offset in firsts]


def add_products(plan, where, firsts, flows, n_late):
    slots, rows, columns = where.shape[0], *flows[0][-1].shape
    arrays, firsts_at = arrays_of(firsts)
    seconds = [x for flow in flows for x in flow]
    smem, hbm = pl.BlockSpec(memory_space=pltpu.SMEM), pl.BlockSpec(memory_space=pltpu.HBM)
    both = pltpu.VMEM((2, rows, columns), jnp.float32)
    return pl.pallas_call(
        functools.partial(
            multiply, firsts_at=firsts_at, n_arrays=len(arrays), n_flows=len(flows), n_late=n_late
        ),
        out_shape=[
            jax.ShapeDtypeStruct((slots, rows, columns), jnp.float32),
            jax.ShapeDtypeStruct((LATE,), jnp.int32),
        ],
        in_specs=[hbm] * (2 + len(arrays) + len(seconds)),
        out_specs=[pl.BlockSpec(memory_space=pltpu.VMEM), smem],
        scratch_shapes=[
            both,
            both,
            pltpu.VMEM((len(firsts) + len(flows), PAD, LANES * slots), jnp.float32),
            pltpu.VMEM((PAD, LANES), jnp.int32),
            pltpu.SMEM((PAD, LANES), jnp.int32),
            pltpu.SMEM((4 * slots * slots * len(flows),), jnp.int32),
            pltpu.SMEM(plan.shape, jnp.int32),
            pltpu.SMEM(where.shape, jnp.int32),
            pltpu.SemaphoreType.DMA((1,)),
            pltpu.SemaphoreType.DMA((2,)),
        ],
        cost_estimate=pl.CostEstimate(
            flops=12 * len(seconds) * rows * columns * columns,
            bytes_accessed=4 * rows * columns * (slots + 2 * len(seconds)),
            transcendentals=0,
        ),
        compiler_params=pltpu.CompilerParams(vmem_limit_bytes=60 * 1024 * 1024),
    )(plan, where, *arrays, *seconds)


def add_late_products(late, firsts, seconds, sums):
    slots, rows, columns = sums.shape
    arrays, _ = arrays_of(firsts)
    where_it_is = pl.BlockSpec(memory_space=pltpu.HBM)
    blocks = [*arrays, *seconds, sums]
    pair = pltpu.VMEM((slots, rows, columns), jnp.float32)
    return pl.pallas_call(
        functools.partial(multiply_late, n_arrays=len(arrays), n_second=len(seconds)),
        out_shape=jax.ShapeDtypeStruct((slots, rows, columns), jnp.float32),
        in_specs=[where_it_is] * (1 + len(blocks)),
        out_specs=where_it_is,
        scratch_shapes=[
            pair,
            pltpu.VMEM((rows, columns), jnp.float32),
            pair,
            pltpu.SMEM((LATE,), jnp.int32),
            pltpu.SemaphoreType.DMA((slots + 2,)),
        ],
        input_output_aliases={len(blocks): 0},
        cost_estimate=pl.CostEstimate(
            flops=12 * len(seconds) * rows * columns * columns,
            bytes_accessed=4 * rows * columns * (slots + 2 * len(seconds)),
            transcendentals=0,
        ),
        compiler_params=pltpu.CompilerParams(vmem_limit_bytes=8 * 1024 * 1024),
    )(late, *blocks)


def both_cores(wide, a_chip, where, n):
    here = lax.dynamic_update_slice(wide, a_chip, (a_chip.shape[0], 0, 0))
    swap = lambda x: lax.ppermute(x, "row", [(p, p ^ 1) for p in range(n)])
    return here, lax.cond(where[0] >= 0, swap, jnp.zeros_like, here)


def by_four(a, a_cells, b, b_cells, where, n):
    parts = list(tagged(b, b_cells, True))
    slots = range(len(parts))
    last = slots[-1]
    j, i = np.meshgrid(np.arange(n), np.arange(n), indexing="ij")
    a, parts[0] = lax.optimization_barrier((a, parts[0]))
    a, wide = tagged_twice(a, a_cells)
    a_chip = lax.ppermute(a, "row", [(p, p ^ 2) for p in range(n)])

    tiles = [np.tile(np.arange(n), (n, 1))]
    for down_tiles, up_tiles in zip(origins(DOWN, n), origins(UP, n)):
        tiles += [down_tiles, up_tiles]
    plan = [np.where((tile >= 0) & ((tile - i - j) % n < STEPS), tile ^ j, -1) for tile in tiles]
    assert not np.any((plan[-2] >= 0) & (plan[-1] >= 0))
    plan = jnp.asarray(np.stack(plan, -1), jnp.int32)[lax.axis_index("row"), lax.axis_index("col")]

    flows = [parts]
    down, up = list(parts), list(parts)
    for stage in range(len(DOWN)):
        for s in slots:
            if (stage, s) == (1, last):
                up[s], plan = lax.optimization_barrier((up[s], plan))
            down[s], up[s] = move(down[s], DOWN[stage], n), move(up[s], UP[stage], n)
        flows += [list(down), list(up)]
    here, there = both_cores(wide, a_chip, where, n)
    firsts = [(here, 0), (there, 0), (here, len(parts)), (there, len(parts))]
    late_blocks = [flow.pop() for flow in flows[-2:]]
    sums, late = add_products(plan, where, firsts, flows, 2)
    return add_late_products(late, firsts, late_blocks, sums)


def by_any(a, a_cells, b, b_cells, where, n):
    (a,), parts = tagged(a, a_cells, False), tagged(b, b_cells, True)
    firsts, flows = [], []
    here = [(j, i) for j in range(n) for i in range(n)]
    for step in range(STEPS):
        from_row = [(((i + j + step) % n) * n + i, j * n + i) for j, i in here]
        from_col = [(j * n + (i + j + step) % n, j * n + i) for j, i in here]
        firsts.append((lax.ppermute(a, AXES, from_row), 0))
        flows.append([lax.ppermute(part, AXES, from_col) for part in parts])
    return add_products(jnp.arange(STEPS, dtype=jnp.int32), where, firsts, flows, 0)[0]


def on_device(a_blocks, first_factor_cell_index, b_blocks, second_factor_cell_index, c_where):
    n = lax.axis_size("row")
    blocks = (a_blocks, first_factor_cell_index, b_blocks, second_factor_cell_index, c_where)
    return (by_four if n == 4 else by_any)(*(x[0, 0] for x in blocks), n)[None, None]


def solution(mesh):
    return jax.shard_map(
        on_device,
        mesh=mesh,
        in_specs=(
            P(("groups", "col"), "row", None, None, None),
            P(("groups", "col"), "row", None),
            P(("groups", "col"), "row", None, None, None),
            P(("groups", "col"), "row", None),
            P(("groups", "col"), "row", None),
        ),
        out_specs=P(("groups", "col"), "row", None, None, None),
        check_vma=False,
    )
```
